512 devices in a mesh: member: 8 (over y_hi, core), space: 64 (over x, y_lo, z).
Axes of the slice: x: 4, y: 8 (y_hi: 4, y_lo: 2; y = y_hi * 2 + y_lo), z: 8, core: 2. Of those that a mesh axis runs over, the one named last changes fastest.
Arguments:
- mean_logk: float32 [256, 128, 256], P('space'), may hold values from -2.5 to 2.5
- perturbation: float32 [8, 256, 128, 256], P('member', 'space'), may hold values from -2.5 to 2.5
- start_conc: float32 [8, 256, 128, 256], P('member', 'space'), may hold values from 0 to 1
- source_mask: int32 [8, 256, 128, 256], P('member', 'space'), may hold values 0 or 1
- control_x: int32 [128, 256], replicated, may hold values from 0 to 255
- observed: float32 [8, 8], P('member'), may hold values from -4 to 4
Outputs:
- updated_logk: float32 [256, 128, 256], P('space')
- misfit: float32 [], replicated
The draws below stay inside these ranges and needn't reach their ends.
All inputs are finite; a program needn't handle non-finite values. No bound on the sum of `source_mask` on one device may be relied on, other than what follows from the above.
Results may differ from the reference program's by a relative error of at most 0.0003.
Values sent between devices are 32-bit elements; how exact they have to be, the bound alone decides.
A program may use at most 64 MiB of HBM per device.

```python
import jax
import jax.numpy as jnp
from jax import lax

NY = 128
NZ = 256
NOBS = 8
MEMBERS = 8
NX = 256
COLS = 4096
CELLS = 8388608


def draw_control_x(key, part):
    key = jax.random.fold_in(key, 11)
    return jax.random.randint(key, (NY, NZ), 0, NX).astype(jnp.int32)


def touch_ends(values, rng, low, high):
    extent = values.shape
    index_at = [jax.random.randint(jax.random.fold_in(rng, axis), (), 0, extent[axis]) for axis in range(len(extent))]
    values = values.at[tuple(index_at)].set(low)
    longest = extent.index(max(extent))
    index_at[longest] = (index_at[longest] + 1) % extent[longest]
    return values.at[tuple(index_at)].set(high)


def shard_levels(key, shape, pieces, smallest, largest):
    gain, own = 1.0, jax.random.fold_in(key, 6)
    for axis_at, shards_of in pieces:
        heights = jnp.exp(jax.random.uniform(jax.random.fold_in(own, axis_at), (shards_of,), jnp.float32, smallest / len(pieces), largest / len(pieces)))
        gain = gain * jnp.repeat(heights, shape[axis_at] // shards_of).reshape([-1 if axis == axis_at else 1 for axis in range(len(shape))])
    return gain


def noise(stream_key, dims, width, most, pieces=(), kind=jnp.bfloat16):
    level = shard_levels(stream_key, dims, pieces, -0.22, 0.18) if pieces else 1.0
    drawn = jax.random.normal(stream_key, dims, jnp.float32) * width * level
    return jnp.minimum(jnp.maximum(drawn, -most), most).astype(kind)


def setup_inputs(seed: int = 0) -> dict:
    arg_keys = jax.random.split(jax.random.key(seed), 7)
    mean_logk = noise(arg_keys[0], (NX, NY, NZ), 0.4, 2.5, ((0, 64),), jnp.float32)
    perturbation = noise(arg_keys[1], (MEMBERS, NX, NY, NZ), 0.4, 2.5, ((0, 8), (1, 64)), jnp.float32)
    start_conc = jnp.clip(1.0 * jax.random.uniform(arg_keys[2], (MEMBERS, NX, NY, NZ), jnp.float32) ** shard_levels(arg_keys[2], (MEMBERS, NX, NY, NZ), ((0, 8), (1, 64)), -0.2, 0.2), 0.0, 1.0)
    source_mask = touch_ends((jax.random.randint(arg_keys[3], (MEMBERS, NX, NY, NZ), 0, 4) < 1).astype(jnp.int32), jax.random.fold_in(arg_keys[3], 1), 0, 1)
    control_x = draw_control_x(jax.random.fold_in(arg_keys[6], 71), 0)
    observed = noise(arg_keys[5], (MEMBERS, NOBS), 1.0, 4.0, ((0, 8),), jnp.float32)
    return dict(mean_logk=mean_logk, perturbation=perturbation, start_conc=start_conc, source_mask=source_mask, control_x=control_x, observed=observed)


time_step = 0.015
dissolve_rate = 15.0
descent_rate = 0.5
epsilon = 1e-06

def flow(field, conduct):
    fpad = jnp.pad(field, 1)
    kpad = jnp.pad(conduct, 1)
    total = jnp.zeros_like(field)
    for axis in range(3):
        for offset in (1, -1):
            index = []
            for other in range(3):
                if other == axis:
                    index.append(slice(1 + offset, fpad.shape[other] - 1 + offset))
                else:
                    index.append(slice(1, fpad.shape[other] - 1))
            index = tuple(index)
            total = total + 0.5 * (conduct + kpad[index]) * (fpad[index] - field)
    return total

def transport(conc, conduct, maskf):
    return conc + time_step * flow(conc, conduct) + time_step * dissolve_rate * maskf * (1.0 - conc)

def member_loss(mean_logk, perturb, conc, maskf, control_x, obs):
    conduct = jnp.exp(mean_logk + perturb)
    conc1 = transport(conc, conduct, maskf)
    conc2 = transport(conc1, conduct, maskf)
    select = (jnp.arange(NX, dtype=jnp.int32)[:, None, None] == control_x[None]).astype(jnp.float32)
    column = lax.optimization_barrier(jnp.sum(select * conduct * conc2, axis=0))
    discharge = column.reshape(NOBS, -1).sum(axis=1) / COLS
    resid = discharge - obs
    return (0.5 * COLS * jnp.sum(resid * resid), resid)

def reference(mean_logk, perturbation, start_conc, source_mask, control_x, observed):
    gradient = jnp.zeros_like(mean_logk)
    misfit = jnp.zeros((), jnp.float32)
    for member in range(MEMBERS):
        maskf = source_mask[member].astype(jnp.float32)
        grads, resid = jax.grad(member_loss, has_aux=True)(mean_logk, perturbation[member], start_conc[member], maskf, control_x, observed[member])
        gradient = gradient + grads
        misfit = misfit + 0.5 * jnp.sum(resid * resid)
    misfit = misfit / (MEMBERS * NOBS)
    squares = jnp.sum(gradient * gradient) / CELLS
    updated = mean_logk - descent_rate * gradient / jnp.sqrt(squares + epsilon)
    return (updated, misfit)
```

```python
import jax
import jax.numpy as jnp
from jax import lax
from jax.experimental import pallas as pl
from jax.experimental.pallas import tpu as pltpu
from jax.sharding import PartitionSpec as P

MESH = pl.DeviceIdType.MESH

NOBS = 8
time_step = 0.015
dissolve_rate = 15.0
descent_rate = 0.5
epsilon = 1e-06

HALF = 0.5 * time_step
RATE = time_step * dissolve_rate
NX, NLO, NZ, NHI = 4, 2, 8, 4
SPACE, MEMBERS = NX * NLO * NZ, 2 * NHI
LAYERS, ROWS, LANES = 4, 128, 256
PAD = 8
SEG = ROWS // NOBS
BLOCK = 32
NB = ROWS // BLOCK


def kernel(
    mean_hbm, pert_hbm, conc_hbm, mask_hbm, ctrl_hbm, obs_ref,
    tot_hbm, row_ref,
    mean, pert, mask, ctrl, K, C, U, D, Pf, Q, L1, X, acc, accq, wgt, dlt,
    g, sib, hsum, rs, tot, lo_buf, xz_buf, y_buf, xz2_buf,
    load_sem, halo_s, halo_r, lo_sem, xz_sem, y_sem, xz2_sem, sib_sem, rs_s, rs_r, ag_s, ag_r, sg_s, sg_r, out_sem,
):
    m, s = lax.axis_index("member"), lax.axis_index("space")
    core, h = lax.rem(m, 2), m // 2
    z, yl, x = lax.rem(s, NZ), lax.rem(s // NZ, NLO), s // (NZ * NLO)

    def dev(member, space):
        return {"member": member, "space": space}

    right, left = lax.rem(s + 1, SPACE), lax.rem(s + SPACE - 1, SPACE)
    sibling = dev(m + 1 - 2 * core, s)
    other_lo = dev(m, x * (NZ * NLO) + (1 - yl) * NZ + z)
    xz_peers = []
    for dx in (2, 1, 3, 0):
        for dz in (4, 3, 5, 2, 6, 1, 7, 0):
            if dx or dz:
                px, pz = lax.rem(x + dx, NX), lax.rem(z + dz, NZ)
                xz_peers.append(dev(m, px * (NZ * NLO) + yl * NZ + pz))
    y_peers = []
    for dh in (2, 1, 3, 0):
        for dl in (0, 1):
            for dc in (0, 1):
                if dh or dl or dc:
                    ph, pc = lax.rem(h + dh, NHI), lax.rem(core + dc, 2)
                    pyl = lax.rem(yl + dl, NLO)
                    y_peers.append(dev(ph * 2 + pc, x * (NZ * NLO) + pyl * NZ + z))
    barrier = pltpu.get_barrier_semaphore()
    greet = [dev(m, right), dev(m, left)] + xz_peers + y_peers
    for peer in greet:
        pl.semaphore_signal(barrier, inc=1, device_id=peer, device_id_type=MESH)

    inside = pl.ds(PAD, ROWS)
    edges = (0, LAYERS - 1)
    loads = {}

    def load(name, index, src, dst):
        loads[name] = pltpu.make_async_copy(src, dst, load_sem.at[index])
        loads[name].start()

    for i, l in enumerate(edges):
        load(("m", l), i, mean_hbm.at[l], mean.at[l])
        load(("p", l), 2 + i, pert_hbm.at[0, l], pert.at[l])
    for i, l in enumerate(edges):
        load(("c", l), 4 + i, conc_hbm.at[0, l], C.at[l + 1, inside])
    mid = pl.ds(1, LAYERS - 2)
    load("ctrl", 6, ctrl_hbm, ctrl)
    load("m", 7, mean_hbm.at[mid], mean.at[mid])
    load("p", 8, pert_hbm.at[0, mid], pert.at[mid])
    load("c", 9, conc_hbm.at[0, mid], C.at[pl.ds(2, LAYERS - 2), inside])
    load("mask", 10, mask_hbm.at[0], mask)

    zero_rows = jnp.zeros((LAYERS + 2, PAD, LANES), jnp.float32)
    for ref in (K, C, U, D, Pf, Q, L1, X):
        ref[:, 0:PAD, :] = zero_rows
        ref[:, PAD + ROWS : 2 * PAD + ROWS, :] = zero_rows
    acc[...] = jnp.zeros_like(acc)
    accq[...] = jnp.zeros_like(accq)

    lane = lax.broadcasted_iota(jnp.int32, (BLOCK, LANES), 1)
    first_lane, last_lane = lane == 0, lane == LANES - 1
    wide = BLOCK + 2 * PAD

    def ext_rows(b):
        return pl.ds(pl.multiple_of(b * BLOCK, BLOCK), wide)

    def mid_rows(b):
        return pl.ds(pl.multiple_of(b * BLOCK + PAD, PAD), BLOCK)

    def own_rows(b):
        return pl.ds(pl.multiple_of(b * BLOCK, BLOCK), BLOCK)

    def centre(ext):
        return ext[PAD : PAD + BLOCK]

    def along_y(ext):
        down, up = pltpu.roll(ext, 1, 0), pltpu.roll(ext, wide - 1, 0)
        return centre(down) + centre(up)

    def along_z(v):
        down, up = pltpu.roll(v, 1, 1), pltpu.roll(v, LANES - 1, 1)
        return jnp.where(first_lane, 0.0, down) + jnp.where(last_lane, 0.0, up)

    def in_plane(ext):
        return along_y(ext) + along_z(centre(ext))

    def blocks(body):
        lax.fori_loop(0, NB, lambda b, c: (body(b), c)[1], 0)

    def exp_layer(l):
        def body(b):
            K[l + 1, mid_rows(b), :] = jnp.exp(mean[l, own_rows(b), :] + pert[l, own_rows(b), :])
        blocks(body)

    def select_layer(e):
        where_x = s * LAYERS + (e - 1)

        def body(b):
            U[e, mid_rows(b), :] = jnp.where(ctrl[own_rows(b), :] == where_x, K[e, mid_rows(b), :], 0.0)
        blocks(body)

    def parity_rows(b):
        row = lax.broadcasted_iota(jnp.int32, (wide, LANES), 0) + (b * BLOCK - PAD)
        return lax.rem((row + SEG * 2) // SEG, 2)

    def cross_layer(e):
        def body(b):
            u, k = U[e, ext_rows(b), :], K[e, ext_rows(b), :]
            row = parity_rows(b)
            mine = centre(row) == 0
            even = jnp.where(row == 0, u, 0.0)
            odd = u - even
            k_mid = centre(k)
            from_odd = k_mid * along_y(odd) + along_y(k * odd)
            from_even = k_mid * along_y(even) + along_y(k * even)
            Q[e, mid_rows(b), :] = HALF * jnp.where(mine, from_odd, from_even)
        blocks(body)

    def transport_layer(e):
        def body(b):
            rows, ext, own = mid_rows(b), ext_rows(b), own_rows(b)
            k_ext, c_ext, u_ext = K[e, ext, :], C[e, ext, :], U[e, ext, :]
            k, c, u = centre(k_ext), centre(c_ext), centre(u_ext)
            k0, k1 = K[e - 1, rows, :], K[e + 1, rows, :]
            c0, c1 = C[e - 1, rows, :], C[e + 1, rows, :]
            u0, u1 = U[e - 1, rows, :], U[e + 1, rows, :]
            diag = 6.0 * k + (k0 + k1) + in_plane(k_ext)
            rate = RATE * mask[e - 1, own, :].astype(jnp.float32)
            flow_c = k * (c0 + c1 + in_plane(c_ext)) + (k0 * c0 + k1 * c1) + in_plane(k_ext * c_ext) - c * diag
            first = c + HALF * flow_c + rate * (1.0 - c)
            flow_u = k * (u0 + u1 + in_plane(u_ext)) + (k0 * u0 + k1 * u1) + in_plane(k_ext * u_ext) - u * diag
            adj = u + HALF * flow_u - rate * u
            D[e, rows, :] = first
            Pf[e, rows, :] = adj
            acc[own, :] += adj * first + u * rate
            accq[own, :] += Q[e, rows, :] * first
        blocks(body)

    for l in edges:
        loads[("m", l)].wait()
        loads[("p", l)].wait()
        exp_layer(l)
    for l in edges:
        loads[("c", l)].wait()
    pl.semaphore_wait(barrier, len(greet))

    def halo(fields, first):
        copies = []
        for i, ref in enumerate(fields):
            for j, (src, dst, to) in enumerate(((LAYERS, 0, right), (1, LAYERS + 1, left))):
                n = first + 2 * i + j
                copies.append(
                    pltpu.make_async_remote_copy(
                        src_ref=ref.at[src, inside], dst_ref=ref.at[dst, inside],
                        send_sem=halo_s.at[n], recv_sem=halo_r.at[n],
                        device_id=dev(m, to), device_id_type=MESH,
                    )
                )
                copies[-1].start()
        return copies

    halo_1 = halo((K, C), 0)
    loads["m"].wait()
    loads["p"].wait()
    exp_layer(1)
    exp_layer(2)
    loads["ctrl"].wait()
    for e in range(1, LAYERS + 1):
        select_layer(e)
    for e in range(1, LAYERS + 1):
        cross_layer(e)
    loads["c"].wait()
    loads["mask"].wait()
    transport_layer(2)
    transport_layer(3)

    def clear(refs):
        blank = jnp.zeros((ROWS, LANES), jnp.float32)

        @pl.when(s == 0)
        def _():
            for ref in refs:
                ref[0, PAD : PAD + ROWS, :] = blank

        @pl.when(s == SPACE - 1)
        def _():
            for ref in refs:
                ref[LAYERS + 1, PAD : PAD + ROWS, :] = blank

    for copy in halo_1:
        copy.wait_recv()
    clear((K, C))
    select_layer(0)
    select_layer(LAYERS + 1)
    transport_layer(1)
    transport_layer(LAYERS)
    halo_2 = halo((D, Pf), 4)

    eye = (lax.broadcasted_iota(jnp.int32, (NOBS, 128), 0) == lax.broadcasted_iota(jnp.int32, (NOBS, 128), 1)).astype(jnp.float32)
    sub = lax.broadcasted_iota(jnp.int32, (NOBS, 128), 0)

    def group(ref, r):
        tile = ref[8 * r : 8 * r + 8, :]
        return tile[:, :128] + tile[:, 128:]

    crosses = [group(accq, r) for r in range(2 * NOBS)]
    parts = jnp.zeros((NOBS, 128), jnp.float32)
    for j in range(NOBS):
        a, b = 2 * j, 2 * j + 1
        tile = group(acc, a) + group(acc, b) - crosses[a] - crosses[b]
        if j > 0:
            tile = tile + crosses[a - 1]
        if j < NOBS - 1:
            tile = tile + crosses[b + 1]
        parts = jnp.where(sub == j, jnp.sum(tile, axis=0, keepdims=True), parts)

    def to_row(column):
        return jnp.sum(eye * column, axis=0, keepdims=True)

    def exchange(buf, slot, row, peers, sems):
        buf[slot] = row
        for peer in peers:
            pltpu.make_async_remote_copy(
                src_ref=buf.at[slot], dst_ref=buf.at[slot],
                send_sem=sems.at[0], recv_sem=sems.at[1],
                device_id=peer, device_id_type=MESH,
            ).start()

    def finish(buf, count, sems):
        span = buf.at[pl.ds(0, count)]
        pltpu.make_async_copy(span, span, sems.at[1]).wait()
        pltpu.make_async_copy(span, span, sems.at[0]).wait()
        return jnp.sum(buf[...], axis=0)

    exchange(lo_buf, yl, to_row(jnp.sum(parts, axis=1, keepdims=True)), [other_lo], lo_sem)
    row = finish(lo_buf, 1, lo_sem)
    exchange(xz_buf, x * NZ + z, row, xz_peers, xz_sem)

    for copy in halo_2:
        copy.wait_recv()
    clear((D, Pf))
    cross_layer(0)
    cross_layer(LAYERS + 1)
    row = finish(xz_buf, NX * NZ - 1, xz_sem)

    observed = jnp.zeros((NOBS, 128), jnp.float32)
    for j in range(NOBS):
        observed = jnp.where(sub == j, obs_ref[0, j], observed)
    total_column = jnp.sum(eye * row, axis=1, keepdims=True)
    resid = total_column * (1.0 / (ROWS * LANES // NOBS)) - observed
    misfit = jnp.sum(resid * resid, axis=0, keepdims=True)
    for r in range(2 * NOBS):
        j = r // 2
        other = max(j - 1, 0) if r % 2 == 0 else min(j + 1, NOBS - 1)
        mine = jnp.broadcast_to(resid[j : j + 1], (8, 128))
        delta = jnp.broadcast_to(resid[other : other + 1], (8, 128)) - mine
        for half in (0, 128):
            wgt[8 * r : 8 * r + 8, half : half + 128] = mine
            dlt[8 * r : 8 * r + 8, half : half + 128] = delta

    def weigh_layer(e):
        def body(b):
            rows, own = mid_rows(b), own_rows(b)
            w = wgt[own, :]
            lam2 = w * U[e, rows, :]
            lam1 = w * Pf[e, rows, :] + dlt[own, :] * Q[e, rows, :]
            U[e, rows, :] = lam2
            L1[e, rows, :] = lam1
            X[e, rows, :] = lam2 * D[e, rows, :] + lam1 * C[e, rows, :]
        blocks(body)

    for e in range(LAYERS + 2):
        weigh_layer(e)

    def gradient_block(e, b):
        rows, ext, own = mid_rows(b), ext_rows(b), own_rows(b)

        def near(ref):
            e_ext = ref[e, ext, :]
            return centre(e_ext), ref[e - 1, rows, :] + ref[e + 1, rows, :] + in_plane(e_ext)

        k_ext, d_ext = K[e, ext, :], D[e, ext, :]
        k0, k1 = K[e - 1, rows, :], K[e + 1, rows, :]
        d0, d1 = D[e - 1, rows, :], D[e + 1, rows, :]
        k, d = centre(k_ext), centre(d_ext)
        diag = 6.0 * k + (k0 + k1) + in_plane(k_ext)
        near_d = d0 + d1 + in_plane(d_ext)
        rate = RATE * mask[e - 1, own, :].astype(jnp.float32)
        flow_d = k * near_d + (k0 * d0 + k1 * d1) + in_plane(k_ext * d_ext) - d * diag
        second = d + HALF * flow_d + rate * (1.0 - d)
        lam2, near_lam2 = near(U)
        lam1, near_lam1 = near(L1)
        c, near_c = near(C)
        both, near_both = near(X)
        bracket = near_both + 6.0 * both - lam2 * near_d - d * near_lam2 - lam1 * near_c - c * near_lam1
        g[e - 1, own, :] = lam2 * second - HALF * k * bracket

    half_rows = ROWS // 2
    half_blocks = NB // 2

    def gradient_half(which):
        def body(i, carry):
            gradient_block(i // half_blocks + 1, which * half_blocks + lax.rem(i, half_blocks))
            return carry

        lax.fori_loop(0, LAYERS * half_blocks, body, 0)

    gradient_half(1 - core)
    sib_copy = pltpu.make_async_remote_copy(
        src_ref=g.at[:, pl.ds(pl.multiple_of((1 - core) * half_rows, half_rows), half_rows), :], dst_ref=sib,
        send_sem=sib_sem.at[0], recv_sem=sib_sem.at[1], device_id=sibling, device_id_type=MESH,
    )
    sib_copy.start()
    gradient_half(core)
    sib_copy.wait_recv()

    piece = half_rows // NHI

    def piece_of(chip):
        return pl.ds(pl.multiple_of(chip * piece, piece), piece)

    def add_cores(chip):
        mine = pl.ds(pl.multiple_of(core * half_rows + chip * piece, piece), piece)
        hsum[:, piece_of(chip), :] = g[:, mine, :] + sib[:, piece_of(chip), :]

    scatter = []
    for i, k in enumerate((2, 1, 3)):
        chip = lax.rem(h + k, NHI)
        add_cores(chip)
        scatter.append(
            pltpu.make_async_remote_copy(
                src_ref=hsum.at[:, piece_of(chip), :], dst_ref=rs.at[i],
                send_sem=rs_s.at[i], recv_sem=rs_r.at[i],
                device_id=dev(chip * 2 + core, s), device_id_type=MESH,
            )
        )
        scatter[-1].start()
    add_cores(h)
    for copy in scatter:
        copy.wait_recv()
    total = hsum[:, piece_of(h), :] + rs[0] + rs[1] + rs[2]

    def final_rows(of_core, chip):
        return pl.ds(pl.multiple_of(of_core * half_rows + chip * piece, piece), piece)

    tot[:, final_rows(core, h), :] = total

    def hand_on(chip, i):
        part = tot.at[:, final_rows(core, chip), :]
        copy = pltpu.make_async_remote_copy(
            src_ref=part, dst_ref=part, send_sem=sg_s.at[i], recv_sem=sg_r.at[i],
            device_id=sibling, device_id_type=MESH,
        )
        copy.start()
        return copy

    gather = []
    mine = tot.at[:, final_rows(core, h), :]
    for i, k in enumerate((2, 1, 3)):
        gather.append(
            pltpu.make_async_remote_copy(
                src_ref=mine, dst_ref=mine, send_sem=ag_s.at[i], recv_sem=ag_r.at[i],
                device_id=dev(lax.rem(h + k, NHI) * 2 + core, s), device_id_type=MESH,
            )
        )
        gather[-1].start()
    handed = [hand_on(h, 0)]

    squares = jnp.sum(jnp.sum(total * total, axis=0), axis=0, keepdims=True)
    squares = jnp.sum(squares, axis=1, keepdims=True)
    lane_row = lax.broadcasted_iota(jnp.int32, (1, 128), 1)
    row = jnp.where(lane_row == 0, squares, jnp.where(lane_row == 1, misfit, 0.0))
    exchange(y_buf, yl * MEMBERS + m, row, y_peers, y_sem)
    row = finish(y_buf, MEMBERS * NLO - 1, y_sem)
    exchange(xz2_buf, x * NZ + z, row, xz_peers, xz2_sem)

    for i, k in ((1, 1), (2, 3), (0, 2)):
        gather[i].wait_recv()
        handed.append(hand_on(lax.rem(h + NHI - k, NHI), i + 1))
    for copy in handed:
        copy.wait_recv()
    out = pltpu.make_async_copy(tot, tot_hbm, out_sem)
    out.start()
    row = finish(xz2_buf, NX * NZ - 1, xz2_sem)
    row_ref[...] = row
    for copy in halo_1 + halo_2 + [sib_copy] + scatter + gather + handed:
        copy.wait_send()
    out.wait()


def shards(mean_logk, perturbation, start_conc, source_mask, control_x, observed):
    slab = (LAYERS, ROWS, LANES)
    tall = (LAYERS + 2, ROWS + 2 * PAD, LANES)
    f32 = jnp.float32
    hbm, dma = pl.BlockSpec(memory_space=pl.ANY), pltpu.SemaphoreType.DMA
    piece = ROWS // MEMBERS
    total, row = pl.pallas_call(
        kernel,
        out_shape=(jax.ShapeDtypeStruct(slab, f32), jax.ShapeDtypeStruct((1, 128), f32)),
        in_specs=[hbm] * 5 + [pl.BlockSpec(memory_space=pltpu.SMEM)],
        out_specs=(hbm, pl.BlockSpec(memory_space=pltpu.VMEM)),
        scratch_shapes=[
            pltpu.VMEM(slab, f32), pltpu.VMEM(slab, f32), pltpu.VMEM(slab, jnp.int32), pltpu.VMEM((ROWS, LANES), jnp.int32),
        ]
        + [pltpu.VMEM(tall, f32)] * 8
        + [pltpu.VMEM((ROWS, LANES), f32)] * 4
        + [
            pltpu.VMEM(slab, f32),
            pltpu.VMEM((LAYERS, ROWS // 2, LANES), f32),
            pltpu.VMEM((LAYERS, ROWS // 2, LANES), f32),
            pltpu.VMEM((NHI - 1, LAYERS, piece, LANES), f32),
            pltpu.VMEM(slab, f32),
            pltpu.VMEM((NLO, 1, 128), f32),
            pltpu.VMEM((NX * NZ, 1, 128), f32),
            pltpu.VMEM((MEMBERS * NLO, 1, 128), f32),
            pltpu.VMEM((NX * NZ, 1, 128), f32),
        ]
        + [dma((n,)) for n in (11, 8, 8, 2, 2, 2, 2, 2, 3, 3, 3, 3, 4, 4)]
        + [dma],
        compiler_params=pltpu.CompilerParams(collective_id=0, has_side_effects=True, vmem_limit_bytes=60 << 20),
    )(mean_logk, perturbation, start_conc, source_mask, control_x, observed)
    cells = SPACE * LAYERS * ROWS * LANES
    squares, misfit = row[0, 0], row[0, 1]
    updated = mean_logk - descent_rate * total * lax.rsqrt(squares / cells + epsilon)
    return updated, misfit * (0.5 / (MEMBERS * NOBS * SPACE))


def solution(mesh):
    in_specs = (
        P("space", None, None),
        P("member", "space", None, None),
        P("member", "space", None, None),
        P("member", "space", None, None),
        P(),
        P("member", None),
    )
    out_specs = (P("space", None, None), P())
    return jax.shard_map(shards, mesh=mesh, in_specs=in_specs, out_specs=out_specs, check_vma=False)
```

```python
import jax
import jax.numpy as jnp
from jax import lax
from jax.experimental import pallas as pl
from jax.experimental.pallas import tpu as pltpu
from jax.sharding import PartitionSpec as P

MESH = pl.DeviceIdType.MESH

NOBS = 8
time_step = 0.015
dissolve_rate = 15.0
descent_rate = 0.5
epsilon = 1e-06

HALF = 0.5 * time_step
RATE = time_step * dissolve_rate
NX, NLO, NZ, NHI = 4, 2, 8, 4
SPACE, MEMBERS = NX * NLO * NZ, 2 * NHI
LAYERS, ROWS, LANES = 4, 128, 256
PAD = 8
SEG = ROWS // NOBS
BLOCK = 32
NB = ROWS // BLOCK


def kernel(
    mean_hbm, pert_hbm, conc_hbm, mask_hbm, ctrl_hbm, obs_hbm,
    tot_ref, row_ref,
    mean, pert, mask, ctrl, obs_ref, K, C, U, D, Pf, Dp, G, acc, bnd,
    sib, hsum, rs, tot, lo_buf, xz_buf, y_buf, xz2_buf,
    load_sem, halo_s, halo_r, lo_sem, xz_sem, y_sem, xz2_sem, sib_s, sib_r, rs_s, rs_r, ag_s, ag_r, sg_s, sg_r, out_sem,
):
    m, s = lax.axis_index("member"), lax.axis_index("space")
    core, h = lax.rem(m, 2), m // 2
    z, yl, x = lax.rem(s, NZ), lax.rem(s // NZ, NLO), s // (NZ * NLO)

    def dev(member, space):
        return {"member": member, "space": space}

    right, left = lax.rem(s + 1, SPACE), lax.rem(s + SPACE - 1, SPACE)
    sibling = dev(m + 1 - 2 * core, s)
    other_lo = dev(m, x * (NZ * NLO) + (1 - yl) * NZ + z)
    xz_peers, xzc_peers = [], []
    for dx in (2, 1, 3, 0):
        for dz in (4, 3, 5, 2, 6, 1, 7, 0):
            px, pz = lax.rem(x + dx, NX), lax.rem(z + dz, NZ)
            there = px * (NZ * NLO) + yl * NZ + pz
            if dx or dz:
                xz_peers.append(dev(m, there))
            xzc_peers.append(dev(m + 1 - 2 * core, there))
    xzc_peers += xz_peers
    y_peers = []
    for dh in (2, 1, 3, 0):
        for dl in (0, 1):
            if dh or dl:
                y_peers.append(dev(lax.rem(h + dh, NHI) * 2 + core, x * (NZ * NLO) + lax.rem(yl + dl, NLO) * NZ + z))
    barrier = pltpu.get_barrier_semaphore()
    greet = [dev(m, right), dev(m, left)] + xzc_peers + y_peers
    for peer in greet:
        pl.semaphore_signal(barrier, inc=1, device_id=peer, device_id_type=MESH)

    inside = pl.ds(PAD, ROWS)
    edges = (0, LAYERS - 1)
    loads = {}

    def load(name, index, src, dst):
        loads[name] = pltpu.make_async_copy(src, dst, load_sem.at[index])
        loads[name].start()

    for i, l in enumerate(edges):
        load(("m", l), i, mean_hbm.at[l], mean.at[l])
        load(("p", l), 2 + i, pert_hbm.at[0, l], pert.at[l])
    halves = (pl.ds(0, 128), pl.ds(128, 128))
    for i, l in enumerate(edges):
        for k, lanes in enumerate(halves):
            load(("c", l, k), 4 + 2 * i + k, conc_hbm.at[0, l, :, lanes], C.at[l + 1, k, inside])
    mid = pl.ds(1, LAYERS - 2)
    load("ctrl", 8, ctrl_hbm, ctrl)
    load("m", 9, mean_hbm.at[mid], mean.at[mid])
    load("p", 10, pert_hbm.at[0, mid], pert.at[mid])
    for k, lanes in enumerate(halves):
        load(("c", k), 11 + k, conc_hbm.at[0, mid, :, lanes], C.at[pl.ds(2, LAYERS - 2), k, inside])
    load("mask", 13, mask_hbm.at[0], mask)
    load("obs", 14, obs_hbm, obs_ref)

    zero_rows = jnp.zeros((2, PAD, 128), jnp.float32)
    for ref in (K, C, U, D, Pf):
        for e in range(LAYERS + 2):
            ref[e, :, 0:PAD, :] = zero_rows
            ref[e, :, PAD + ROWS : 2 * PAD + ROWS, :] = zero_rows
    acc[...] = jnp.zeros_like(acc)

    def own_rows(b):
        return pl.ds(pl.multiple_of(b * BLOCK, BLOCK), BLOCK)

    def at(ref, e, b, shift=0):
        start = pl.multiple_of(b * BLOCK, BLOCK) + (PAD + shift)
        return ref[e, :, pl.ds(start, BLOCK), :]

    def put(ref, e, b, value):
        ref[e, :, pl.ds(pl.multiple_of(b * BLOCK + PAD, PAD), BLOCK), :] = value

    def split(v):
        return jnp.stack([v[:, :128], v[:, 128:]])

    def shifts_z(v):
        lane = lax.broadcasted_iota(jnp.int32, v.shape, 2)
        before, after = pltpu.roll(v, 1, 2), pltpu.roll(v, 127, 2)
        zero = jnp.zeros_like(v[0])
        down = jnp.where(lane == 0, jnp.stack([zero, before[0]]), before)
        up = jnp.where(lane == 127, jnp.stack([after[1], zero]), after)
        return down, up

    def neighbours(ref, e, b, beside):
        v = at(ref, e, b)
        return v, [at(ref, n, b) for n in beside] + [at(ref, e, b, -1), at(ref, e, b, 1), *shifts_z(v)]

    def each(layers, body):
        first, step, count = layers

        def run(i, carry):
            body(first + step * (i // NB), lax.rem(i, NB))
            return carry

        lax.fori_loop(0, count * NB, run, 0)

    OUTER, INNER, OWN = (1, LAYERS - 1, 2), (2, 1, LAYERS - 2), (1, 1, LAYERS)

    def conductivity(e, b):
        put(K, e, b, split(jnp.exp(mean[e - 1, own_rows(b), :] + pert[e - 1, own_rows(b), :])))

    def selected(e, b):
        where_x = s * LAYERS + (e - 1)
        put(U, e, b, jnp.where(split(ctrl[own_rows(b), :]) == where_x, at(K, e, b), 0.0))

    def edge_of(e):
        return (e - 1) // (LAYERS - 1)

    def inner_of(e):
        return 2 + edge_of(e) * (LAYERS - 3), edge_of(e) * (LAYERS + 1)

    def rate_of(e, b):
        return RATE * split(mask[e - 1, own_rows(b), :]).astype(jnp.float32)

    def gather_discharge(e, b, first, adj, u):
        acc[:, own_rows(b), :] += adj * first + u * rate_of(e, b)

    def transport_block(e, b, beside):
        k, ks = neighbours(K, e, b, beside)
        c, cs = neighbours(C, e, b, beside)
        u, us = neighbours(U, e, b, beside)
        flow_c, flow_u = jnp.zeros_like(c), jnp.zeros_like(u)
        for kn, cn, un in zip(ks, cs, us):
            face = k + kn
            flow_c, flow_u = flow_c + face * (cn - c), flow_u + face * (un - u)
        rate = rate_of(e, b)
        first = c + HALF * flow_c + rate * (1.0 - c)
        adj = u + HALF * flow_u - rate * u
        put(Pf, e, b, adj)
        return first, adj, u

    def transport_inner(e, b):
        first, adj, u = transport_block(e, b, (e - 1, e + 1))
        put(D, e, b, first)
        gather_discharge(e, b, first, adj, u)

    def transport_outer(e, b):
        Dp[edge_of(e), :, own_rows(b), :] = transport_block(e, b, (inner_of(e)[0],))[0]

    def transport_halo(e, b):
        n = inner_of(e)[1]
        face = HALF * (at(K, e, b) + at(K, n, b))
        u = at(U, e, b)
        first = Dp[edge_of(e), :, own_rows(b), :] + face * (at(C, n, b) - at(C, e, b))
        adj = at(Pf, e, b) + face * (at(U, n, b) - u)
        put(D, e, b, first)
        put(Pf, e, b, adj)
        gather_discharge(e, b, first, adj, u)

    def gradient_block(e, b, beside):
        fields = [neighbours(ref, e, b, beside) for ref in (K, C, U, D, Pf)]
        k, c, u, d, p = (centre for centre, _ in fields)
        flow_d, bracket = jnp.zeros_like(d), jnp.zeros_like(d)
        for kn, cn, un, dn, pn in zip(*(around for _, around in fields)):
            slope = dn - d
            flow_d = flow_d + (k + kn) * slope
            bracket = bracket + ((un - u) * slope + (pn - p) * (cn - c))
        second = d + HALF * flow_d + rate_of(e, b) * (1.0 - d)
        G[e - 1, :, own_rows(b), :] = u * second - HALF * k * bracket

    def gradient_inner(e, b):
        gradient_block(e, b, (e - 1, e + 1))

    def gradient_outer(e, b):
        gradient_block(e, b, (inner_of(e)[0],))

    def gradient_halo(e, b):
        n, own = inner_of(e)[1], own_rows(b)
        k, kn, u, un = at(K, e, b), at(K, n, b), at(U, e, b), at(U, n, b)
        slope = at(C, n, b) - at(C, e, b)
        inside_grid = jnp.where(s == edge_of(e) * (SPACE - 1), 0.0, 1.0)
        dn = (at(D, n, b) - HALF * (k + kn) * slope) * inside_grid
        by_d = (dn - at(D, e, b)) * (u * (k + kn) - k * (un - u))
        by_c = k * (at(Pf, n, b) * inside_grid - at(Pf, e, b)) * slope
        G[e - 1, :, own, :] += HALF * (by_d - by_c)

    SIDES = ((0, -1, 1), (SEG - 1, SEG, SEG - 2))

    def strided(ref, e, row):
        return ref[e, :, pl.ds(PAD + row, NOBS, stride=SEG), :]

    def crossing(e, side):
        own_row, over, _ = side
        return HALF * (strided(K, e, own_row) + strided(K, e, over)) * strided(U, e, over)

    def crossing_terms(e):
        return [crossing(e, side) * strided(D, e, side[0]) for side in SIDES]

    def boundary_gradient(e):
        for i, side in enumerate(SIDES):
            row, over, further = side
            q, k, c = crossing(e, side), strided(K, e, row), strided(C, e, row)
            u_over, c_over, c_further = strided(U, e, over), strided(C, e, over), strided(C, e, further)
            p_over = strided(Pf, e, over) - HALF * (k + strided(K, e, over)) * strided(U, e, row)
            bracket = u_over * (strided(D, e, over) - strided(D, e, row))
            bracket += (p_over - q) * (c_over - c) - q * (c_further - c)
            for n in (e - 1, e + 1):
                bracket += (crossing(n, side) - q) * (strided(C, n, row) - c)
            for qn, cn in zip(shifts_z(q), shifts_z(c)):
                bracket += (qn - q) * (cn - c)
            bnd[e - 1, 2 * i] = -HALF * k * bracket
            bnd[e - 1, 2 * i + 1] = -HALF * strided(K, e, further) * (q * (c - c_further))

    for l in edges:
        loads[("m", l)].wait()
        loads[("p", l)].wait()
    each(OUTER, conductivity)
    for l in edges:
        for k in (0, 1):
            loads[("c", l, k)].wait()
    pl.semaphore_wait(barrier, len(greet))

    def halo(pairs, first):
        copies = []
        for i, (low, high, at_left, at_right) in enumerate(pairs):
            for j, (src, dst, to) in enumerate(((high, at_right, right), (low, at_left, left))):
                n = first + 2 * i + j
                copies.append(
                    pltpu.make_async_remote_copy(
                        src_ref=src, dst_ref=dst, send_sem=halo_s.at[n], recv_sem=halo_r.at[n],
                        device_id=dev(m, to), device_id_type=MESH,
                    )
                )
                copies[-1].start()
        return copies

    def layers_of(ref):
        return tuple(ref.at[e, :, inside] for e in (1, LAYERS, LAYERS + 1, 0))

    halo_1 = halo((layers_of(K), layers_of(C)), 0)
    loads["m"].wait()
    loads["p"].wait()
    each(INNER, conductivity)
    loads["ctrl"].wait()
    each(OWN, selected)
    for k in (0, 1):
        loads[("c", k)].wait()
    loads["mask"].wait()
    loads["obs"].wait()
    each(OUTER, transport_outer)
    halo_2 = halo(((Dp.at[0], Dp.at[1], *layers_of(D)[2:]),), 4)
    each(INNER, transport_inner)
    cross_in = [crossing_terms(e) for e in range(2, LAYERS)]

    def clear(refs):
        blank = jnp.zeros((2, ROWS, 128), jnp.float32)

        @pl.when(s == 0)
        def _():
            for ref in refs:
                ref[0, :, PAD : PAD + ROWS, :] = blank

        @pl.when(s == SPACE - 1)
        def _():
            for ref in refs:
                ref[LAYERS + 1, :, PAD : PAD + ROWS, :] = blank

    for copy in halo_1:
        copy.wait_recv()
    clear((K, C))
    each((0, LAYERS + 1, 2), selected)
    each(OUTER, transport_halo)

    eye = (lax.broadcasted_iota(jnp.int32, (NOBS, 128), 0) == lax.broadcasted_iota(jnp.int32, (NOBS, 128), 1)).astype(jnp.float32)
    sub = lax.broadcasted_iota(jnp.int32, (NOBS, 128), 0)
    parts = acc[:, pl.ds(0, NOBS, stride=SEG), :]
    for i in range(1, SEG):
        parts = parts + acc[:, pl.ds(i, NOBS, stride=SEG), :]
    cross_all = cross_in + [crossing_terms(1), crossing_terms(LAYERS)]
    lower, upper = (sum(terms[i] for terms in cross_all) for i in (0, 1))
    parts = parts - lower - upper + pltpu.roll(lower, NOBS - 1, 1) + pltpu.roll(upper, 1, 1)
    column = jnp.sum(parts[0] + parts[1], axis=1, keepdims=True)

    def to_row(column):
        return jnp.sum(eye * column, axis=0, keepdims=True)

    def exchange(buf, slot, row, peers, sems):
        buf[slot] = row
        for peer in peers:
            pltpu.make_async_remote_copy(
                src_ref=buf.at[slot], dst_ref=buf.at[slot],
                send_sem=sems.at[0], recv_sem=sems.at[1],
                device_id=peer, device_id_type=MESH,
            ).start()

    def finish(buf, count, sems):
        span = buf.at[pl.ds(0, count)]
        pltpu.make_async_copy(span, span, sems.at[1]).wait()
        pltpu.make_async_copy(span, span, sems.at[0]).wait()
        return jnp.sum(buf[...], axis=0)

    exchange(lo_buf, yl, to_row(column), [other_lo], lo_sem)
    row = finish(lo_buf, 1, lo_sem)
    exchange(xz_buf, x * NZ + z, row, xz_peers, xz_sem)
    halo_2 += halo((layers_of(Pf),), 6)

    each(INNER, gradient_inner)
    each(OUTER, gradient_outer)
    for e in range(2, LAYERS):
        boundary_gradient(e)
    for copy in halo_2:
        copy.wait_recv()
    each(OUTER, gradient_halo)
    boundary_gradient(1)
    boundary_gradient(LAYERS)
    row = finish(xz_buf, NX * NZ - 1, xz_sem)

    observed = jnp.zeros((NOBS, 128), jnp.float32)
    for j in range(NOBS):
        observed = jnp.where(sub == j, obs_ref[0, j], observed)
    total_column = jnp.sum(eye * row, axis=1, keepdims=True)
    resid = total_column * (1.0 / (ROWS * LANES // NOBS)) - observed
    misfit = jnp.sum(resid * resid, axis=0, keepdims=True)
    below = jnp.where(sub == 0, 0.0, pltpu.roll(resid, 1, 0) - resid)
    above = jnp.where(sub == NOBS - 1, 0.0, pltpu.roll(resid, NOBS - 1, 0) - resid)
    deltas = (below, above)

    def weigh(l, carry):
        for half in (0, 1):
            for j in range(NOBS):
                rows = pl.ds(j * SEG, SEG)
                G[l, half, rows, :] = G[l, half, rows, :] * jnp.broadcast_to(resid[j : j + 1], (SEG, 128))
            for i, (row, _, further) in enumerate(SIDES):
                for k, r in enumerate((row, further)):
                    where = pl.ds(r, NOBS, stride=SEG)
                    G[l, half, where, :] = G[l, half, where, :] + deltas[i] * bnd[l, 2 * i + k, half]
        return carry

    lax.fori_loop(0, LAYERS, weigh, 0)

    half_rows = ROWS // 2
    piece = half_rows // NHI

    def piece_of(chip):
        return pl.ds(pl.multiple_of(chip * piece, piece), piece)

    def rows_of(of_core, chip):
        return pl.ds(pl.multiple_of(of_core * half_rows + chip * piece, piece), piece)

    order = (2, 1, 3, 0)
    cores = []
    for i, k in enumerate(order):
        chip = lax.rem(h + k, NHI)
        cores.append(
            pltpu.make_async_remote_copy(
                src_ref=G.at[:, :, rows_of(1 - core, chip), :], dst_ref=sib.at[:, :, piece_of(chip), :],
                send_sem=sib_s.at[i], recv_sem=sib_r.at[i], device_id=sibling, device_id_type=MESH,
            )
        )
        cores[-1].start()
    scatter = []
    for i, k in enumerate(order):
        chip = lax.rem(h + k, NHI)
        cores[i].wait_recv()
        hsum[:, :, piece_of(chip), :] = G[:, :, rows_of(core, chip), :] + sib[:, :, piece_of(chip), :]
        if k:
            scatter.append(
                pltpu.make_async_remote_copy(
                    src_ref=hsum.at[:, :, piece_of(chip), :], dst_ref=rs.at[i],
                    send_sem=rs_s.at[i], recv_sem=rs_r.at[i],
                    device_id=dev(chip * 2 + core, s), device_id_type=MESH,
                )
            )
            scatter[-1].start()
    for copy in scatter:
        copy.wait_recv()
    total = hsum[:, :, piece_of(h), :] + rs[0] + rs[1] + rs[2]
    tot[:, :, rows_of(core, h), :] = total

    def hand_on(chip, i):
        part = tot.at[:, :, rows_of(core, chip), :]
        copy = pltpu.make_async_remote_copy(
            src_ref=part, dst_ref=part, send_sem=sg_s.at[i], recv_sem=sg_r.at[i],
            device_id=sibling, device_id_type=MESH,
        )
        copy.start()
        return copy

    gather = []
    mine = tot.at[:, :, rows_of(core, h), :]
    for i, k in enumerate((2, 1, 3)):
        gather.append(
            pltpu.make_async_remote_copy(
                src_ref=mine, dst_ref=mine, send_sem=ag_s.at[i], recv_sem=ag_r.at[i],
                device_id=dev(lax.rem(h + k, NHI) * 2 + core, s), device_id_type=MESH,
            )
        )
        gather[-1].start()
    handed = [hand_on(h, 0)]

    squares = jnp.sum(jnp.sum(total * total, axis=(0, 1)), axis=0, keepdims=True)
    squares = jnp.sum(squares, axis=1, keepdims=True)
    lane_row = lax.broadcasted_iota(jnp.int32, (1, 128), 1)
    row = jnp.where(lane_row == 0, squares, jnp.where(lane_row == 1, misfit, 0.0))
    exchange(xz2_buf, (x * NZ + z) * 2 + core, row, xzc_peers, xz2_sem)
    row = finish(xz2_buf, 2 * NX * NZ - 1, xz2_sem)
    exchange(y_buf, h * NLO + yl, row, y_peers, y_sem)

    for i, k in ((1, 1), (2, 3), (0, 2)):
        gather[i].wait_recv()
        handed.append(hand_on(lax.rem(h + NHI - k, NHI), i + 1))
    for copy in handed:
        copy.wait_recv()
    out = pltpu.make_async_copy(tot, tot_ref, out_sem)
    out.start()
    for copy in halo_1 + halo_2 + cores + scatter + gather + handed:
        copy.wait_send()
    row = finish(y_buf, NHI * NLO - 1, y_sem)
    row_ref[...] = row
    out.wait()


def update_kernel(row_ref, mean_ref, tot_ref, out_ref, misfit_ref):
    squares = jnp.full((8, 128), row_ref[0, 0])
    scale = descent_rate * lax.rsqrt(squares * (1.0 / (SPACE * LAYERS * ROWS * LANES)) + epsilon)
    for l in range(LAYERS):
        for r in range(0, ROWS, 8):
            for k in (0, 1):
                lanes = slice(128 * k, 128 * k + 128)
                out_ref[l, r : r + 8, lanes] = mean_ref[l, r : r + 8, lanes] - scale * tot_ref[l, k, r : r + 8, :]
    misfit_ref[0, 0] = row_ref[0, 1] * (0.5 / (MEMBERS * NOBS * SPACE))


def shards(mean_logk, perturbation, start_conc, source_mask, control_x, observed):
    slab = (LAYERS, ROWS, LANES)
    halved = (LAYERS, 2, ROWS, 128)
    tall = (LAYERS + 2, 2, ROWS + 2 * PAD, 128)
    f32 = jnp.float32
    dma = pltpu.SemaphoreType.DMA
    hbm, anywhere = pl.BlockSpec(memory_space=pltpu.HBM), pl.BlockSpec(memory_space=pl.ANY)
    vmem, smem = pl.BlockSpec(memory_space=pltpu.VMEM), pl.BlockSpec(memory_space=pltpu.SMEM)
    piece = ROWS // MEMBERS
    pinned = [
        pltpu.with_memory_space_constraint(v, pltpu.HBM) for v in (mean_logk, perturbation, start_conc, source_mask, control_x, observed)
    ]
    total, row = pl.pallas_call(
        kernel,
        out_shape=(jax.ShapeDtypeStruct(halved, f32), jax.ShapeDtypeStruct((1, 128), f32)),
        in_specs=[hbm] * 6,
        out_specs=(anywhere, vmem),
        scratch_shapes=[
            pltpu.VMEM(slab, f32), pltpu.VMEM(slab, f32), pltpu.VMEM(slab, jnp.int32), pltpu.VMEM((ROWS, LANES), jnp.int32),
            pltpu.SMEM((1, NOBS), f32),
        ]
        + [pltpu.VMEM(tall, f32)] * 5
        + [
            pltpu.VMEM((2, 2, ROWS, 128), f32),
            pltpu.VMEM(halved, f32),
            pltpu.VMEM((2, ROWS, 128), f32),
            pltpu.VMEM((LAYERS, 4, 2, NOBS, 128), f32),
            pltpu.VMEM((LAYERS, 2, ROWS // 2, 128), f32),
            pltpu.VMEM((LAYERS, 2, ROWS // 2, 128), f32),
            pltpu.VMEM((NHI - 1, LAYERS, 2, piece, 128), f32),
            pltpu.VMEM(halved, f32),
            pltpu.VMEM((NLO, 1, 128), f32),
            pltpu.VMEM((NX * NZ, 1, 128), f32),
            pltpu.VMEM((NHI * NLO, 1, 128), f32),
            pltpu.VMEM((2 * NX * NZ, 1, 128), f32),
        ]
        + [dma((n,)) for n in (15, 8, 8, 2, 2, 2, 2, 4, 4, 3, 3, 3, 3, 4, 4)]
        + [dma],
        compiler_params=pltpu.CompilerParams(collective_id=0, has_side_effects=True, vmem_limit_bytes=24 << 20),
        name="step",
    )(*pinned)
    updated, misfit = pl.pallas_call(
        update_kernel,
        out_shape=(jax.ShapeDtypeStruct(slab, f32), jax.ShapeDtypeStruct((1, 1), f32)),
        in_specs=[smem, vmem, vmem],
        out_specs=(vmem, smem),
        compiler_params=pltpu.CompilerParams(vmem_limit_bytes=8 << 20),
        name="update",
    )(row, mean_logk, total)
    return updated, misfit[0, 0]


def solution(mesh):
    in_specs = (
        P("space", None, None),
        P("member", "space", None, None),
        P("member", "space", None, None),
        P("member", "space", None, None),
        P(),
        P("member", None),
    )
    out_specs = (P("space", None, None), P())
    return jax.shard_map(shards, mesh=mesh, in_specs=in_specs, out_specs=out_specs, check_vma=False)
```

```python
import jax
import jax.numpy as jnp
from jax import lax
from jax.experimental import pallas as pl
from jax.experimental.pallas import tpu as pltpu
from jax.sharding import PartitionSpec as P

MESH = pl.DeviceIdType.MESH

NOBS = 8
time_step = 0.015
dissolve_rate = 15.0
descent_rate = 0.5
epsilon = 1e-06

HALF = 0.5 * time_step
RATE = time_step * dissolve_rate
NX, NLO, NZ, NHI = 4, 2, 8, 4
SPACE, MEMBERS = NX * NLO * NZ, 2 * NHI
LAYERS, ROWS, LANES = 4, 128, 256
PAD = 8
SEG = ROWS // NOBS
BLOCK = 32
NB = ROWS // BLOCK


def kernel(
    mean_hbm, pert_hbm, conc_hbm, mask_hbm, ctrl_hbm, obs_hbm,
    tot_ref, row_ref,
    mean, pert, mask, ctrl, obs_ref, K, C, U, D, Pf, Dp, G, acc, bnd,
    sib, hsum, rs, tot, space_buf, y_buf, plane_buf,
    load_sem, halo_s, halo_r, space_sem, y_sem, plane_sem, sib_s, sib_r, rs_s, rs_r, ag_s, ag_r, sg_s, sg_r, out_sem, relay,
):
    m, s = lax.axis_index("member"), lax.axis_index("space")
    core, h = lax.rem(m, 2), m // 2
    z, yl, x = lax.rem(s, NZ), lax.rem(s // NZ, NLO), s // (NZ * NLO)

    def dev(member, space):
        return {"member": member, "space": space}

    right, left = lax.rem(s + 1, SPACE), lax.rem(s + SPACE - 1, SPACE)
    sibling = dev(m + 1 - 2 * core, s)

    def place(dx, dl, dz):
        return (lax.rem(x + dx, NX) * NLO + lax.rem(yl + dl, NLO)) * NZ + lax.rem(z + dz, NZ)

    far_x, far_z, far_h = (2, 1, 3, 0), (4, 3, 5, 2, 6, 1, 7, 0), (2, 1, 3, 0)
    plane = [(dx, dz) for dx in far_x for dz in far_z]
    space_peers = [dev(m, place(dx, dl, dz)) for dx, dz in plane for dl in (1, 0) if dx or dl or dz]
    plane_peers = [dev(m + 1 - 2 * core, place(dx, 0, dz)) for dx, dz in plane]
    plane_peers += [dev(m, place(dx, 0, dz)) for dx, dz in plane if dx or dz]
    y_peers = [dev(lax.rem(h + dh, NHI) * 2 + core, place(0, dl, 0)) for dh in far_h for dl in (1, 0) if dh or dl]

    def greet(semaphore, peers):
        for peer in peers:
            pl.semaphore_signal(semaphore, inc=1, device_id=peer, device_id_type=MESH)

    z_ring = [dev(m, place(0, 0, dz)) for dz in far_z if dz]
    x_ring = [dev(m, place(dx, 0, 0)) for dx in far_x if dx]
    h_near = [dev(lax.rem(h + dh, NHI) * 2 + core, s) for dh in (1, NHI - 1)]
    beside = [dev(m, place(0, 1, 0)), sibling]
    near = [dev(m, right), dev(m, left)] + z_ring + x_ring + h_near + beside
    barrier = pltpu.get_barrier_semaphore()
    greet(barrier, near)

    inside = pl.ds(PAD, ROWS)
    edges = (0, LAYERS - 1)
    loads = {}

    def load(name, index, src, dst):
        loads[name] = pltpu.make_async_copy(src, dst, load_sem.at[index])
        loads[name].start()

    for i, l in enumerate(edges):
        load(("m", l), i, mean_hbm.at[l], mean.at[l])
        load(("p", l), 2 + i, pert_hbm.at[0, l], pert.at[l])
    halves = (pl.ds(0, 128), pl.ds(128, 128))
    for i, l in enumerate(edges):
        for k, lanes in enumerate(halves):
            load(("c", l, k), 4 + 2 * i + k, conc_hbm.at[0, l, :, lanes], C.at[l + 1, k, inside])
    mid = pl.ds(1, LAYERS - 2)
    load("ctrl", 8, ctrl_hbm, ctrl)
    load("m", 9, mean_hbm.at[mid], mean.at[mid])
    load("p", 10, pert_hbm.at[0, mid], pert.at[mid])
    for k, lanes in enumerate(halves):
        load(("c", k), 11 + k, conc_hbm.at[0, mid, :, lanes], C.at[pl.ds(2, LAYERS - 2), k, inside])
    load("mask", 13, mask_hbm.at[0], mask)
    load("obs", 14, obs_hbm, obs_ref)

    zero_rows = jnp.zeros((2, PAD, 128), jnp.float32)
    for ref in (K, C, U, D, Pf):
        for e in range(LAYERS + 2):
            ref[e, :, 0:PAD, :] = zero_rows
            ref[e, :, PAD + ROWS : 2 * PAD + ROWS, :] = zero_rows
    acc[...] = jnp.zeros_like(acc)

    def own_rows(b):
        return pl.ds(pl.multiple_of(b * BLOCK, BLOCK), BLOCK)

    def at(ref, e, b, shift=0):
        start = pl.multiple_of(b * BLOCK, BLOCK) + (PAD + shift)
        return ref[e, :, pl.ds(start, BLOCK), :]

    def put(ref, e, b, value):
        ref[e, :, pl.ds(pl.multiple_of(b * BLOCK + PAD, PAD), BLOCK), :] = value

    def split(v):
        return jnp.stack([v[:, :128], v[:, 128:]])

    def shifts_z(v):
        lane = lax.broadcasted_iota(jnp.int32, v.shape, 2)
        before, after = pltpu.roll(v, 1, 2), pltpu.roll(v, 127, 2)
        zero = jnp.zeros_like(v[0])
        down = jnp.where(lane == 0, jnp.stack([zero, before[0]]), before)
        up = jnp.where(lane == 127, jnp.stack([after[1], zero]), after)
        return down, up

    def neighbours(ref, e, b, beside):
        v = at(ref, e, b)
        return v, [at(ref, n, b) for n in beside] + [at(ref, e, b, -1), at(ref, e, b, 1), *shifts_z(v)]

    def each(layers, body):
        first, step, count = layers

        def run(i, carry):
            body(first + step * (i // NB), lax.rem(i, NB))
            return carry

        lax.fori_loop(0, count * NB, run, 0)

    OUTER, INNER, OWN = (1, LAYERS - 1, 2), (2, 1, LAYERS - 2), (1, 1, LAYERS)

    def conductivity(e, b):
        put(K, e, b, split(jnp.exp(mean[e - 1, own_rows(b), :] + pert[e - 1, own_rows(b), :])))

    def selected(e, b):
        where_x = s * LAYERS + (e - 1)
        put(U, e, b, jnp.where(split(ctrl[own_rows(b), :]) == where_x, at(K, e, b), 0.0))

    def edge_of(e):
        return (e - 1) // (LAYERS - 1)

    def inner_of(e):
        return 2 + edge_of(e) * (LAYERS - 3), edge_of(e) * (LAYERS + 1)

    def rate_of(e, b):
        return RATE * split(mask[e - 1, own_rows(b), :]).astype(jnp.float32)

    def gather_discharge(e, b, first, adj, u):
        acc[:, own_rows(b), :] += adj * first + u * rate_of(e, b)

    def transport_block(e, b, beside):
        k, ks = neighbours(K, e, b, beside)
        c, cs = neighbours(C, e, b, beside)
        u, us = neighbours(U, e, b, beside)
        flow_c, flow_u = jnp.zeros_like(c), jnp.zeros_like(u)
        for kn, cn, un in zip(ks, cs, us):
            face = k + kn
            flow_c, flow_u = flow_c + face * (cn - c), flow_u + face * (un - u)
        rate = rate_of(e, b)
        first = c + HALF * flow_c + rate * (1.0 - c)
        adj = u + HALF * flow_u - rate * u
        put(Pf, e, b, adj)
        return first, adj, u

    def transport_inner(e, b):
        first, adj, u = transport_block(e, b, (e - 1, e + 1))
        put(D, e, b, first)
        gather_discharge(e, b, first, adj, u)

    def transport_outer(e, b):
        Dp[edge_of(e), :, own_rows(b), :] = transport_block(e, b, (inner_of(e)[0],))[0]

    def transport_halo(e, b):
        n = inner_of(e)[1]
        face = HALF * (at(K, e, b) + at(K, n, b))
        u = at(U, e, b)
        first = Dp[edge_of(e), :, own_rows(b), :] + face * (at(C, n, b) - at(C, e, b))
        adj = at(Pf, e, b) + face * (at(U, n, b) - u)
        put(D, e, b, first)
        put(Pf, e, b, adj)
        gather_discharge(e, b, first, adj, u)

    def gradient_block(e, b, beside):
        fields = [neighbours(ref, e, b, beside) for ref in (K, C, U, D, Pf)]
        k, c, u, d, p = (centre for centre, _ in fields)
        flow_d, bracket = jnp.zeros_like(d), jnp.zeros_like(d)
        for kn, cn, un, dn, pn in zip(*(around for _, around in fields)):
            slope = dn - d
            flow_d = flow_d + (k + kn) * slope
            bracket = bracket + ((un - u) * slope + (pn - p) * (cn - c))
        second = d + HALF * flow_d + rate_of(e, b) * (1.0 - d)
        G[e - 1, :, own_rows(b), :] = u * second - HALF * k * bracket

    def gradient_inner(e, b):
        gradient_block(e, b, (e - 1, e + 1))

    def gradient_outer(e, b):
        gradient_block(e, b, (inner_of(e)[0],))

    def gradient_halo(e, b):
        n, own = inner_of(e)[1], own_rows(b)
        k, kn, u, un = at(K, e, b), at(K, n, b), at(U, e, b), at(U, n, b)
        slope = at(C, n, b) - at(C, e, b)
        inside_grid = jnp.where(s == edge_of(e) * (SPACE - 1), 0.0, 1.0)
        dn = (at(D, n, b) - HALF * (k + kn) * slope) * inside_grid
        by_d = (dn - at(D, e, b)) * (u * (k + kn) - k * (un - u))
        by_c = k * (at(Pf, n, b) * inside_grid - at(Pf, e, b)) * slope
        G[e - 1, :, own, :] += HALF * (by_d - by_c)

    SIDES = ((0, -1, 1), (SEG - 1, SEG, SEG - 2))

    def strided(ref, e, row):
        return ref[e, :, pl.ds(PAD + row, NOBS, stride=SEG), :]

    def crossing(e, side):
        own_row, over, _ = side
        return HALF * (strided(K, e, own_row) + strided(K, e, over)) * strided(U, e, over)

    def crossing_terms(e):
        return [crossing(e, side) * strided(D, e, side[0]) for side in SIDES]

    def boundary_gradient(e):
        for i, side in enumerate(SIDES):
            row, over, further = side
            q, k, c = crossing(e, side), strided(K, e, row), strided(C, e, row)
            u_over, c_over, c_further = strided(U, e, over), strided(C, e, over), strided(C, e, further)
            p_over = strided(Pf, e, over) - HALF * (k + strided(K, e, over)) * strided(U, e, row)
            bracket = u_over * (strided(D, e, over) - strided(D, e, row))
            bracket += (p_over - q) * (c_over - c) - q * (c_further - c)
            for n in (e - 1, e + 1):
                bracket += (crossing(n, side) - q) * (strided(C, n, row) - c)
            for qn, cn in zip(shifts_z(q), shifts_z(c)):
                bracket += (qn - q) * (cn - c)
            bnd[e - 1, 2 * i] = -HALF * k * bracket
            bnd[e - 1, 2 * i + 1] = -HALF * strided(K, e, further) * (q * (c - c_further))

    for l in edges:
        loads[("m", l)].wait()
        loads[("p", l)].wait()
    each(OUTER, conductivity)
    for l in edges:
        for k in (0, 1):
            loads[("c", l, k)].wait()
    pl.semaphore_wait(barrier, len(near))
    greet(relay.at[0], x_ring + h_near)

    def halo(pairs, first):
        copies = []
        for i, (low, high, at_left, at_right) in enumerate(pairs):
            for j, (src, dst, to) in enumerate(((high, at_right, right), (low, at_left, left))):
                n = first + 2 * i + j
                copies.append(
                    pltpu.make_async_remote_copy(
                        src_ref=src, dst_ref=dst, send_sem=halo_s.at[n], recv_sem=halo_r.at[n],
                        device_id=dev(m, to), device_id_type=MESH,
                    )
                )
                copies[-1].start()
        return copies

    def layers_of(ref):
        return tuple(ref.at[e, :, inside] for e in (1, LAYERS, LAYERS + 1, 0))

    halo_1 = halo((layers_of(K), layers_of(C)), 0)
    loads["m"].wait()
    loads["p"].wait()
    each(INNER, conductivity)
    pl.semaphore_wait(relay.at[0], len(x_ring + h_near))
    greet(relay.at[1], beside)
    loads["ctrl"].wait()
    each(OWN, selected)
    for k in (0, 1):
        loads[("c", k)].wait()
    loads["mask"].wait()
    loads["obs"].wait()
    each(OUTER, transport_outer)
    halo_2 = halo(((Dp.at[0], Dp.at[1], *layers_of(D)[2:]),), 4)
    each(INNER, transport_inner)
    cross_in = [crossing_terms(e) for e in range(2, LAYERS)]

    def clear(refs):
        blank = jnp.zeros((2, ROWS, 128), jnp.float32)

        @pl.when(s == 0)
        def _():
            for ref in refs:
                ref[0, :, PAD : PAD + ROWS, :] = blank

        @pl.when(s == SPACE - 1)
        def _():
            for ref in refs:
                ref[LAYERS + 1, :, PAD : PAD + ROWS, :] = blank

    for copy in halo_1:
        copy.wait_recv()
    clear((K, C))
    each((0, LAYERS + 1, 2), selected)
    each(OUTER, transport_halo)

    eye = (lax.broadcasted_iota(jnp.int32, (NOBS, 128), 0) == lax.broadcasted_iota(jnp.int32, (NOBS, 128), 1)).astype(jnp.float32)
    sub = lax.broadcasted_iota(jnp.int32, (NOBS, 128), 0)
    parts = acc[:, pl.ds(0, NOBS, stride=SEG), :]
    for i in range(1, SEG):
        parts = parts + acc[:, pl.ds(i, NOBS, stride=SEG), :]
    cross_all = cross_in + [crossing_terms(1), crossing_terms(LAYERS)]
    lower, upper = (sum(terms[i] for terms in cross_all) for i in (0, 1))
    parts = parts - lower - upper + pltpu.roll(lower, NOBS - 1, 1) + pltpu.roll(upper, 1, 1)
    column = jnp.sum(parts[0] + parts[1], axis=1, keepdims=True)

    def to_row(column):
        return jnp.sum(eye * column, axis=0, keepdims=True)

    def exchange(buf, slot, row, peers, sems):
        buf[slot] = row
        for peer in peers:
            pltpu.make_async_remote_copy(
                src_ref=buf.at[slot], dst_ref=buf.at[slot],
                send_sem=sems.at[0], recv_sem=sems.at[1],
                device_id=peer, device_id_type=MESH,
            ).start()

    def finish(buf, count, sems):
        span = buf.at[pl.ds(0, count)]
        pltpu.make_async_copy(span, span, sems.at[1]).wait()
        pltpu.make_async_copy(span, span, sems.at[0]).wait()
        return jnp.sum(buf[...], axis=0)

    pl.semaphore_wait(relay.at[1], len(beside))
    exchange(space_buf, s, to_row(column), space_peers, space_sem)
    halo_2 += halo((layers_of(Pf),), 6)

    each(INNER, gradient_inner)
    each(OUTER, gradient_outer)
    for e in range(2, LAYERS):
        boundary_gradient(e)
    for copy in halo_2:
        copy.wait_recv()
    each(OUTER, gradient_halo)
    boundary_gradient(1)
    boundary_gradient(LAYERS)
    row = finish(space_buf, SPACE - 1, space_sem)

    observed = jnp.zeros((NOBS, 128), jnp.float32)
    for j in range(NOBS):
        observed = jnp.where(sub == j, obs_ref[0, j], observed)
    total_column = jnp.sum(eye * row, axis=1, keepdims=True)
    resid = total_column * (1.0 / (ROWS * LANES // NOBS)) - observed
    misfit = jnp.sum(resid * resid, axis=0, keepdims=True)
    below = jnp.where(sub == 0, 0.0, pltpu.roll(resid, 1, 0) - resid)
    above = jnp.where(sub == NOBS - 1, 0.0, pltpu.roll(resid, NOBS - 1, 0) - resid)
    deltas = (below, above)

    def weigh(l, carry):
        for half in (0, 1):
            for j in range(NOBS):
                rows = pl.ds(j * SEG, SEG)
                G[l, half, rows, :] = G[l, half, rows, :] * jnp.broadcast_to(resid[j : j + 1], (SEG, 128))
            for i, (row, _, further) in enumerate(SIDES):
                for k, r in enumerate((row, further)):
                    where = pl.ds(r, NOBS, stride=SEG)
                    G[l, half, where, :] = G[l, half, where, :] + deltas[i] * bnd[l, 2 * i + k, half]
        return carry

    lax.fori_loop(0, LAYERS, weigh, 0)

    half_rows = ROWS // 2
    piece = half_rows // NHI

    def piece_of(chip):
        return pl.ds(pl.multiple_of(chip * piece, piece), piece)

    def rows_of(of_core, chip):
        return pl.ds(pl.multiple_of(of_core * half_rows + chip * piece, piece), piece)

    order = (2, 1, 3, 0)
    cores = []
    for i, k in enumerate(order):
        chip = lax.rem(h + k, NHI)
        cores.append(
            pltpu.make_async_remote_copy(
                src_ref=G.at[:, :, rows_of(1 - core, chip), :], dst_ref=sib.at[:, :, piece_of(chip), :],
                send_sem=sib_s.at[i], recv_sem=sib_r.at[i], device_id=sibling, device_id_type=MESH,
            )
        )
        cores[-1].start()
    scatter = []
    for i, k in enumerate(order):
        chip = lax.rem(h + k, NHI)
        cores[i].wait_recv()
        hsum[:, :, piece_of(chip), :] = G[:, :, rows_of(core, chip), :] + sib[:, :, piece_of(chip), :]
        if k:
            scatter.append(
                pltpu.make_async_remote_copy(
                    src_ref=hsum.at[:, :, piece_of(chip), :], dst_ref=rs.at[i],
                    send_sem=rs_s.at[i], recv_sem=rs_r.at[i],
                    device_id=dev(chip * 2 + core, s), device_id_type=MESH,
                )
            )
            scatter[-1].start()
    for copy in scatter:
        copy.wait_recv()
    total = hsum[:, :, piece_of(h), :] + rs[0] + rs[1] + rs[2]
    tot[:, :, rows_of(core, h), :] = total

    def hand_on(chip, i):
        part = tot.at[:, :, rows_of(core, chip), :]
        copy = pltpu.make_async_remote_copy(
            src_ref=part, dst_ref=part, send_sem=sg_s.at[i], recv_sem=sg_r.at[i],
            device_id=sibling, device_id_type=MESH,
        )
        copy.start()
        return copy

    gather = []
    mine = tot.at[:, :, rows_of(core, h), :]
    for i, k in enumerate((2, 1, 3)):
        gather.append(
            pltpu.make_async_remote_copy(
                src_ref=mine, dst_ref=mine, send_sem=ag_s.at[i], recv_sem=ag_r.at[i],
                device_id=dev(lax.rem(h + k, NHI) * 2 + core, s), device_id_type=MESH,
            )
        )
        gather[-1].start()
    handed = [hand_on(h, 0)]

    squares = jnp.sum(jnp.sum(total * total, axis=(0, 1)), axis=0, keepdims=True)
    squares = jnp.sum(squares, axis=1, keepdims=True)
    lane_row = lax.broadcasted_iota(jnp.int32, (1, 128), 1)
    row = jnp.where(lane_row == 0, squares, jnp.where(lane_row == 1, misfit, 0.0))
    exchange(plane_buf, (x * NZ + z) * 2 + core, row, plane_peers, plane_sem)
    row = finish(plane_buf, 2 * NX * NZ - 1, plane_sem)
    exchange(y_buf, h * NLO + yl, row, y_peers, y_sem)

    for i, k in ((1, 1), (2, 3), (0, 2)):
        gather[i].wait_recv()
        handed.append(hand_on(lax.rem(h + NHI - k, NHI), i + 1))
    for copy in handed:
        copy.wait_recv()
    out = pltpu.make_async_copy(tot, tot_ref, out_sem)
    out.start()
    for copy in halo_1 + halo_2 + cores + scatter + gather + handed:
        copy.wait_send()
    row = finish(y_buf, NHI * NLO - 1, y_sem)
    row_ref[...] = row
    out.wait()


def update_kernel(row_ref, mean_ref, tot_ref, out_ref, misfit_ref):
    squares = jnp.full((8, 128), row_ref[0, 0])
    scale = descent_rate * lax.rsqrt(squares * (1.0 / (SPACE * LAYERS * ROWS * LANES)) + epsilon)
    for l in range(LAYERS):
        for r in range(0, ROWS, 8):
            for k in (0, 1):
                lanes = slice(128 * k, 128 * k + 128)
                out_ref[l, r : r + 8, lanes] = mean_ref[l, r : r + 8, lanes] - scale * tot_ref[l, k, r : r + 8, :]
    misfit_ref[0, 0] = row_ref[0, 1] * (0.5 / (MEMBERS * NOBS * SPACE))


def shards(mean_logk, perturbation, start_conc, source_mask, control_x, observed):
    slab = (LAYERS, ROWS, LANES)
    halved = (LAYERS, 2, ROWS, 128)
    tall = (LAYERS + 2, 2, ROWS + 2 * PAD, 128)
    f32 = jnp.float32
    dma = pltpu.SemaphoreType.DMA
    hbm, anywhere = pl.BlockSpec(memory_space=pltpu.HBM), pl.BlockSpec(memory_space=pl.ANY)
    vmem, smem = pl.BlockSpec(memory_space=pltpu.VMEM), pl.BlockSpec(memory_space=pltpu.SMEM)
    piece = ROWS // MEMBERS
    pinned = [
        pltpu.with_memory_space_constraint(v, pltpu.HBM) for v in (mean_logk, perturbation, start_conc, source_mask, control_x, observed)
    ]
    total, row = pl.pallas_call(
        kernel,
        out_shape=(jax.ShapeDtypeStruct(halved, f32), jax.ShapeDtypeStruct((1, 128), f32)),
        in_specs=[hbm] * 6,
        out_specs=(anywhere, vmem),
        scratch_shapes=[
            pltpu.VMEM(slab, f32), pltpu.VMEM(slab, f32), pltpu.VMEM(slab, jnp.int32), pltpu.VMEM((ROWS, LANES), jnp.int32),
            pltpu.SMEM((1, NOBS), f32),
        ]
        + [pltpu.VMEM(tall, f32)] * 5
        + [
            pltpu.VMEM((2, 2, ROWS, 128), f32),
            pltpu.VMEM(halved, f32),
            pltpu.VMEM((2, ROWS, 128), f32),
            pltpu.VMEM((LAYERS, 4, 2, NOBS, 128), f32),
            pltpu.VMEM((LAYERS, 2, ROWS // 2, 128), f32),
            pltpu.VMEM((LAYERS, 2, ROWS // 2, 128), f32),
            pltpu.VMEM((NHI - 1, LAYERS, 2, piece, 128), f32),
            pltpu.VMEM(halved, f32),
            pltpu.VMEM((SPACE, 1, 128), f32),
            pltpu.VMEM((NHI * NLO, 1, 128), f32),
            pltpu.VMEM((2 * NX * NZ, 1, 128), f32),
        ]
        + [dma((n,)) for n in (15, 8, 8, 2, 2, 2, 4, 4, 3, 3, 3, 3, 4, 4)]
        + [dma, pltpu.SemaphoreType.REGULAR((2,))],
        compiler_params=pltpu.CompilerParams(collective_id=0, has_side_effects=True, vmem_limit_bytes=24 << 20),
        name="step",
    )(*pinned)
    updated, misfit = pl.pallas_call(
        update_kernel,
        out_shape=(jax.ShapeDtypeStruct(slab, f32), jax.ShapeDtypeStruct((1, 1), f32)),
        in_specs=[smem, vmem, vmem],
        out_specs=(vmem, smem),
        compiler_params=pltpu.CompilerParams(vmem_limit_bytes=8 << 20),
        name="update",
    )(row, mean_logk, total)
    return updated, misfit[0, 0]


def solution(mesh):
    in_specs = (
        P("space", None, None),
        P("member", "space", None, None),
        P("member", "space", None, None),
        P("member", "space", None, None),
        P(),
        P("member", None),
    )
    out_specs = (P("space", None, None), P())
    return jax.shard_map(shards, mesh=mesh, in_specs=in_specs, out_specs=out_specs, check_vma=False)
```

```python
import jax
import jax.numpy as jnp
from jax import lax
from jax.experimental import pallas as pl
from jax.experimental.pallas import tpu as pltpu
from jax.sharding import PartitionSpec as P

MESH = pl.DeviceIdType.MESH

NOBS = 8
time_step = 0.015
dissolve_rate = 15.0
descent_rate = 0.5
epsilon = 1e-06

HALF = 0.5 * time_step
RATE = time_step * dissolve_rate
NX, NLO, NZ, NHI = 4, 2, 8, 4
SPACE, MEMBERS = NX * NLO * NZ, 2 * NHI
LAYERS, ROWS, LANES = 4, 128, 256
PAD = 8
SEG = ROWS // NOBS
BLOCK = 32
NB = ROWS // BLOCK


def kernel(
    mean_hbm, pert_hbm, conc_hbm, mask_hbm, ctrl_hbm, obs_hbm,
    tot_ref, row_ref,
    mean, pert, mask, ctrl, obs_ref, K, C, U, D, Pf, Dp, G, acc, bnd,
    sib, hsum, rs, tot, space_buf, y_buf, plane_buf,
    load_sem, halo_s, halo_r, space_sem, y_sem, plane_sem, sib_s, sib_r, rs_s, rs_r, ag_s, ag_r, sg_s, sg_r, out_sem, relay,
):
    m, s = lax.axis_index("member"), lax.axis_index("space")
    core, h = lax.rem(m, 2), m // 2
    z, yl, x = lax.rem(s, NZ), lax.rem(s // NZ, NLO), s // (NZ * NLO)

    def dev(member, space):
        return {"member": member, "space": space}

    right, left = lax.rem(s + 1, SPACE), lax.rem(s + SPACE - 1, SPACE)
    sibling = dev(m + 1 - 2 * core, s)

    def place(dx, dl, dz):
        return (lax.rem(x + dx, NX) * NLO + lax.rem(yl + dl, NLO)) * NZ + lax.rem(z + dz, NZ)

    far_x, far_z, far_h = (2, 1, 3, 0), (4, 3, 5, 2, 6, 1, 7, 0), (2, 1, 3, 0)
    plane = [(dx, dz) for dx in far_x for dz in far_z]
    space_peers = [dev(m, place(dx, dl, dz)) for dx, dz in plane for dl in (1, 0) if dx or dl or dz]
    plane_peers = [dev(m + 1 - 2 * core, place(dx, 0, dz)) for dx, dz in plane]
    plane_peers += [dev(m, place(dx, 0, dz)) for dx, dz in plane if dx or dz]
    y_peers = [dev(lax.rem(h + dh, NHI) * 2 + core, place(0, dl, 0)) for dh in far_h for dl in (1, 0) if dh or dl]

    def greet(semaphore, peers):
        for peer in peers:
            pl.semaphore_signal(semaphore, inc=1, device_id=peer, device_id_type=MESH)

    z_ring = [dev(m, place(0, 0, dz)) for dz in far_z if dz]
    x_ring = [dev(m, place(dx, 0, 0)) for dx in far_x if dx]
    h_near = [dev(lax.rem(h + dh, NHI) * 2 + core, s) for dh in (1, NHI - 1)]
    beside = [dev(m, place(0, 1, 0)), sibling]
    near = [dev(m, right), dev(m, left)] + z_ring + x_ring + h_near + beside
    inside = pl.ds(PAD, ROWS)
    edges = (0, LAYERS - 1)
    loads = {}

    def load(name, index, src, dst):
        loads[name] = pltpu.make_async_copy(src, dst, load_sem.at[index])
        loads[name].start()

    barrier = pltpu.get_barrier_semaphore()
    greet(barrier, near)
    for i, l in enumerate(edges):
        load(("m", l), i, mean_hbm.at[l], mean.at[l])
        load(("p", l), 2 + i, pert_hbm.at[0, l], pert.at[l])
    halves = (pl.ds(0, 128), pl.ds(128, 128))
    pl.semaphore_wait(barrier, len(near))

    def halo(pairs, first):
        copies = []
        for i, (low, high, at_left, at_right) in enumerate(pairs):
            for j, (src, dst, to) in enumerate(((high, at_right, right), (low, at_left, left))):
                n = first + 2 * i + j
                copies.append(
                    pltpu.make_async_remote_copy(
                        src_ref=src, dst_ref=dst, send_sem=halo_s.at[n], recv_sem=halo_r.at[n],
                        device_id=dev(m, to), device_id_type=MESH,
                    )
                )
                copies[-1].start()
        return copies

    def layers_of(ref):
        return tuple(ref.at[e, :, inside] for e in (1, LAYERS, LAYERS + 1, 0))

    halo_1 = halo(
        [
            (*(conc_hbm.at[0, l, :, lanes] for l in edges), C.at[LAYERS + 1, k, inside], C.at[0, k, inside])
            for k, lanes in enumerate(halves)
        ],
        0,
    )
    greet(relay.at[0], x_ring + h_near)

    mid = pl.ds(1, LAYERS - 2)
    load("ctrl", 8, ctrl_hbm, ctrl)
    load("m", 9, mean_hbm.at[mid], mean.at[mid])
    load("p", 10, pert_hbm.at[0, mid], pert.at[mid])
    for i, l in enumerate(edges):
        for k, lanes in enumerate(halves):
            load(("c", l, k), 4 + 2 * i + k, conc_hbm.at[0, l, :, lanes], C.at[l + 1, k, inside])
    for k, lanes in enumerate(halves):
        load(("c", k), 11 + k, conc_hbm.at[0, mid, :, lanes], C.at[pl.ds(2, LAYERS - 2), k, inside])
    load("mask", 13, mask_hbm.at[0], mask)
    load("obs", 14, obs_hbm, obs_ref)

    def own_rows(b):
        return pl.ds(pl.multiple_of(b * BLOCK, BLOCK), BLOCK)

    def at(ref, e, b, shift=0):
        start = pl.multiple_of(b * BLOCK, BLOCK) + (PAD + shift)
        return ref[e, :, pl.ds(start, BLOCK), :]

    def put(ref, e, b, value):
        ref[e, :, pl.ds(pl.multiple_of(b * BLOCK + PAD, PAD), BLOCK), :] = value

    def split(v):
        return jnp.stack([v[:, :128], v[:, 128:]])

    def shifts_z(v):
        lane = lax.broadcasted_iota(jnp.int32, v.shape, 2)
        before, after = pltpu.roll(v, 1, 2), pltpu.roll(v, 127, 2)
        zero = jnp.zeros_like(v[0])
        down = jnp.where(lane == 0, jnp.stack([zero, before[0]]), before)
        up = jnp.where(lane == 127, jnp.stack([after[1], zero]), after)
        return down, up

    def neighbours(ref, e, b, beside):
        v = at(ref, e, b)
        return v, [at(ref, n, b) for n in beside] + [at(ref, e, b, -1), at(ref, e, b, 1), *shifts_z(v)]

    def each(layers, body):
        first, step, count = layers

        def run(i, carry):
            body(first + step * (i // NB), lax.rem(i, NB))
            return carry

        lax.fori_loop(0, count * NB, run, 0)

    OUTER, INNER, OWN = (1, LAYERS - 1, 2), (2, 1, LAYERS - 2), (1, 1, LAYERS)

    def conductivity(e, b):
        put(K, e, b, split(jnp.exp(mean[e - 1, own_rows(b), :] + pert[e - 1, own_rows(b), :])))

    def selected(e, b):
        where_x = s * LAYERS + (e - 1)
        put(U, e, b, jnp.where(split(ctrl[own_rows(b), :]) == where_x, at(K, e, b), 0.0))

    def edge_of(e):
        return (e - 1) // (LAYERS - 1)

    def inner_of(e):
        return 2 + edge_of(e) * (LAYERS - 3), edge_of(e) * (LAYERS + 1)

    def rate_of(e, b):
        return RATE * split(mask[e - 1, own_rows(b), :]).astype(jnp.float32)

    def gather_discharge(e, b, first, adj, u):
        acc[:, own_rows(b), :] += adj * first + u * rate_of(e, b)

    def transport_block(e, b, beside):
        k, ks = neighbours(K, e, b, beside)
        c, cs = neighbours(C, e, b, beside)
        u, us = neighbours(U, e, b, beside)
        flow_c, flow_u = jnp.zeros_like(c), jnp.zeros_like(u)
        for kn, cn, un in zip(ks, cs, us):
            face = k + kn
            flow_c, flow_u = flow_c + face * (cn - c), flow_u + face * (un - u)
        rate = rate_of(e, b)
        first = c + HALF * flow_c + rate * (1.0 - c)
        adj = u + HALF * flow_u - rate * u
        put(Pf, e, b, adj)
        return first, adj, u

    def transport_inner(e, b):
        first, adj, u = transport_block(e, b, (e - 1, e + 1))
        put(D, e, b, first)
        gather_discharge(e, b, first, adj, u)

    def transport_outer(e, b):
        Dp[edge_of(e), :, own_rows(b), :] = transport_block(e, b, (inner_of(e)[0],))[0]

    def transport_halo(e, b):
        n = inner_of(e)[1]
        face = HALF * (at(K, e, b) + at(K, n, b))
        u = at(U, e, b)
        first = Dp[edge_of(e), :, own_rows(b), :] + face * (at(C, n, b) - at(C, e, b))
        adj = at(Pf, e, b) + face * (at(U, n, b) - u)
        put(D, e, b, first)
        put(Pf, e, b, adj)
        gather_discharge(e, b, first, adj, u)

    def gradient_block(e, b, beside):
        fields = [neighbours(ref, e, b, beside) for ref in (K, C, U, D, Pf)]
        k, c, u, d, p = (centre for centre, _ in fields)
        flow_d, bracket = jnp.zeros_like(d), jnp.zeros_like(d)
        for kn, cn, un, dn, pn in zip(*(around for _, around in fields)):
            slope = dn - d
            flow_d = flow_d + (k + kn) * slope
            bracket = bracket + ((un - u) * slope + (pn - p) * (cn - c))
        second = d + HALF * flow_d + rate_of(e, b) * (1.0 - d)
        G[e - 1, :, own_rows(b), :] = u * second - HALF * k * bracket

    def gradient_inner(e, b):
        gradient_block(e, b, (e - 1, e + 1))

    def gradient_outer(e, b):
        gradient_block(e, b, (inner_of(e)[0],))

    def gradient_halo(e, b):
        n, own = inner_of(e)[1], own_rows(b)
        k, kn, u, un = at(K, e, b), at(K, n, b), at(U, e, b), at(U, n, b)
        slope = at(C, n, b) - at(C, e, b)
        inside_grid = jnp.where(s == edge_of(e) * (SPACE - 1), 0.0, 1.0)
        dn = (at(D, n, b) - HALF * (k + kn) * slope) * inside_grid
        by_d = (dn - at(D, e, b)) * (u * (k + kn) - k * (un - u))
        by_c = k * (at(Pf, n, b) * inside_grid - at(Pf, e, b)) * slope
        G[e - 1, :, own, :] += HALF * (by_d - by_c)

    SIDES = ((0, -1, 1), (SEG - 1, SEG, SEG - 2))

    def strided(ref, e, row):
        return ref[e, :, pl.ds(PAD + row, NOBS, stride=SEG), :]

    def crossing(e, side):
        own_row, over, _ = side
        return HALF * (strided(K, e, own_row) + strided(K, e, over)) * strided(U, e, over)

    def crossing_terms(e):
        return [crossing(e, side) * strided(D, e, side[0]) for side in SIDES]

    def boundary_gradient(e):
        for i, side in enumerate(SIDES):
            row, over, further = side
            q, k, c = crossing(e, side), strided(K, e, row), strided(C, e, row)
            u_over, c_over, c_further = strided(U, e, over), strided(C, e, over), strided(C, e, further)
            p_over = strided(Pf, e, over) - HALF * (k + strided(K, e, over)) * strided(U, e, row)
            bracket = u_over * (strided(D, e, over) - strided(D, e, row))
            bracket += (p_over - q) * (c_over - c) - q * (c_further - c)
            for n in (e - 1, e + 1):
                bracket += (crossing(n, side) - q) * (strided(C, n, row) - c)
            for qn, cn in zip(shifts_z(q), shifts_z(c)):
                bracket += (qn - q) * (cn - c)
            bnd[e - 1, 2 * i] = -HALF * k * bracket
            bnd[e - 1, 2 * i + 1] = -HALF * strided(K, e, further) * (q * (c - c_further))

    for l in edges:
        loads[("m", l)].wait()
        loads[("p", l)].wait()
    each(OUTER, conductivity)
    halo_1 += halo((layers_of(K),), 4)

    zero_rows = jnp.zeros((2, PAD, 128), jnp.float32)
    for ref in (K, C, U, D, Pf):
        for e in range(LAYERS + 2):
            ref[e, :, 0:PAD, :] = zero_rows
            ref[e, :, PAD + ROWS : 2 * PAD + ROWS, :] = zero_rows
    acc[...] = jnp.zeros_like(acc)
    loads["m"].wait()
    loads["p"].wait()
    each(INNER, conductivity)
    pl.semaphore_wait(relay.at[0], len(x_ring + h_near))
    greet(relay.at[1], beside)
    loads["ctrl"].wait()
    each(OWN, selected)
    for l in edges:
        for k in (0, 1):
            loads[("c", l, k)].wait()
    for k in (0, 1):
        loads[("c", k)].wait()
    loads["mask"].wait()
    loads["obs"].wait()
    each(OUTER, transport_outer)
    each(INNER, transport_inner)
    for copy in halo_1:
        copy.wait_send()
    halo_2 = halo(((Dp.at[0], Dp.at[1], *layers_of(D)[2:]),), 6)
    cross_in = [crossing_terms(e) for e in range(2, LAYERS)]

    def clear(refs):
        blank = jnp.zeros((2, ROWS, 128), jnp.float32)

        @pl.when(s == 0)
        def _():
            for ref in refs:
                ref[0, :, PAD : PAD + ROWS, :] = blank

        @pl.when(s == SPACE - 1)
        def _():
            for ref in refs:
                ref[LAYERS + 1, :, PAD : PAD + ROWS, :] = blank

    for copy in halo_1:
        copy.wait_recv()
    clear((K, C))
    each((0, LAYERS + 1, 2), selected)
    each(OUTER, transport_halo)

    eye = (lax.broadcasted_iota(jnp.int32, (NOBS, 128), 0) == lax.broadcasted_iota(jnp.int32, (NOBS, 128), 1)).astype(jnp.float32)
    sub = lax.broadcasted_iota(jnp.int32, (NOBS, 128), 0)
    parts = acc[:, pl.ds(0, NOBS, stride=SEG), :]
    for i in range(1, SEG):
        parts = parts + acc[:, pl.ds(i, NOBS, stride=SEG), :]
    cross_all = cross_in + [crossing_terms(1), crossing_terms(LAYERS)]
    lower, upper = (sum(terms[i] for terms in cross_all) for i in (0, 1))
    parts = parts - lower - upper + pltpu.roll(lower, NOBS - 1, 1) + pltpu.roll(upper, 1, 1)
    column = jnp.sum(parts[0] + parts[1], axis=1, keepdims=True)

    def to_row(column):
        return jnp.sum(eye * column, axis=0, keepdims=True)

    def exchange(buf, slot, row, peers, sems):
        buf[slot] = row
        for peer in peers:
            pltpu.make_async_remote_copy(
                src_ref=buf.at[slot], dst_ref=buf.at[slot],
                send_sem=sems.at[0], recv_sem=sems.at[1],
                device_id=peer, device_id_type=MESH,
            ).start()

    def finish(buf, count, sems):
        span = buf.at[pl.ds(0, count)]
        pltpu.make_async_copy(span, span, sems.at[1]).wait()
        pltpu.make_async_copy(span, span, sems.at[0]).wait()
        return jnp.sum(buf[...], axis=0)

    pl.semaphore_wait(relay.at[1], len(beside))
    exchange(space_buf, s, to_row(column), space_peers, space_sem)
    halo_2 += halo((layers_of(Pf),), 8)

    each(INNER, gradient_inner)
    each(OUTER, gradient_outer)
    for e in range(2, LAYERS):
        boundary_gradient(e)
    for copy in halo_2:
        copy.wait_recv()
    each(OUTER, gradient_halo)
    boundary_gradient(1)
    boundary_gradient(LAYERS)
    row = finish(space_buf, SPACE - 1, space_sem)

    observed = jnp.zeros((NOBS, 128), jnp.float32)
    for j in range(NOBS):
        observed = jnp.where(sub == j, obs_ref[0, j], observed)
    total_column = jnp.sum(eye * row, axis=1, keepdims=True)
    resid = total_column * (1.0 / (ROWS * LANES // NOBS)) - observed
    misfit = jnp.sum(resid * resid, axis=0, keepdims=True)
    below = jnp.where(sub == 0, 0.0, pltpu.roll(resid, 1, 0) - resid)
    above = jnp.where(sub == NOBS - 1, 0.0, pltpu.roll(resid, NOBS - 1, 0) - resid)
    deltas = (below, above)

    def weigh(l, carry):
        for half in (0, 1):
            for j in range(NOBS):
                rows = pl.ds(j * SEG, SEG)
                G[l, half, rows, :] = G[l, half, rows, :] * jnp.broadcast_to(resid[j : j + 1], (SEG, 128))
            for i, (row, _, further) in enumerate(SIDES):
                for k, r in enumerate((row, further)):
                    where = pl.ds(r, NOBS, stride=SEG)
                    G[l, half, where, :] = G[l, half, where, :] + deltas[i] * bnd[l, 2 * i + k, half]
        return carry

    lax.fori_loop(0, LAYERS, weigh, 0)

    half_rows = ROWS // 2
    piece = half_rows // NHI

    def piece_of(chip):
        return pl.ds(pl.multiple_of(chip * piece, piece), piece)

    def rows_of(of_core, chip):
        return pl.ds(pl.multiple_of(of_core * half_rows + chip * piece, piece), piece)

    order = (2, 1, 3, 0)
    cores = []
    for i, k in enumerate(order):
        chip = lax.rem(h + k, NHI)
        cores.append(
            pltpu.make_async_remote_copy(
                src_ref=G.at[:, :, rows_of(1 - core, chip), :], dst_ref=sib.at[:, :, piece_of(chip), :],
                send_sem=sib_s.at[i], recv_sem=sib_r.at[i], device_id=sibling, device_id_type=MESH,
            )
        )
        cores[-1].start()
    scatter = []
    for i, k in enumerate(order):
        chip = lax.rem(h + k, NHI)
        cores[i].wait_recv()
        hsum[:, :, piece_of(chip), :] = G[:, :, rows_of(core, chip), :] + sib[:, :, piece_of(chip), :]
        if k:
            scatter.append(
                pltpu.make_async_remote_copy(
                    src_ref=hsum.at[:, :, piece_of(chip), :], dst_ref=rs.at[i],
                    send_sem=rs_s.at[i], recv_sem=rs_r.at[i],
                    device_id=dev(chip * 2 + core, s), device_id_type=MESH,
                )
            )
            scatter[-1].start()
    for copy in scatter:
        copy.wait_recv()
    total = hsum[:, :, piece_of(h), :] + rs[0] + rs[1] + rs[2]
    tot[:, :, rows_of(core, h), :] = total

    def hand_on(chip, i):
        part = tot.at[:, :, rows_of(core, chip), :]
        copy = pltpu.make_async_remote_copy(
            src_ref=part, dst_ref=part, send_sem=sg_s.at[i], recv_sem=sg_r.at[i],
            device_id=sibling, device_id_type=MESH,
        )
        copy.start()
        return copy

    gather = []
    mine = tot.at[:, :, rows_of(core, h), :]
    for i, k in enumerate((2, 1, 3)):
        gather.append(
            pltpu.make_async_remote_copy(
                src_ref=mine, dst_ref=mine, send_sem=ag_s.at[i], recv_sem=ag_r.at[i],
                device_id=dev(lax.rem(h + k, NHI) * 2 + core, s), device_id_type=MESH,
            )
        )
        gather[-1].start()
    handed = [hand_on(h, 0)]

    squares = jnp.sum(jnp.sum(total * total, axis=(0, 1)), axis=0, keepdims=True)
    squares = jnp.sum(squares, axis=1, keepdims=True)
    lane_row = lax.broadcasted_iota(jnp.int32, (1, 128), 1)
    row = jnp.where(lane_row == 0, squares, jnp.where(lane_row == 1, misfit, 0.0))
    exchange(plane_buf, (x * NZ + z) * 2 + core, row, plane_peers, plane_sem)
    row = finish(plane_buf, 2 * NX * NZ - 1, plane_sem)
    exchange(y_buf, h * NLO + yl, row, y_peers, y_sem)

    for i, k in ((1, 1), (2, 3), (0, 2)):
        gather[i].wait_recv()
        handed.append(hand_on(lax.rem(h + NHI - k, NHI), i + 1))
    for copy in handed:
        copy.wait_recv()
    out = pltpu.make_async_copy(tot, tot_ref, out_sem)
    out.start()
    for copy in halo_2 + cores + scatter + gather + handed:
        copy.wait_send()
    row = finish(y_buf, NHI * NLO - 1, y_sem)
    row_ref[...] = row
    out.wait()


def update_kernel(row_ref, mean_ref, tot_ref, out_ref, misfit_ref):
    lane = lax.broadcasted_iota(jnp.int32, (1, 128), 1)
    squares = jnp.broadcast_to(jnp.sum(jnp.where(lane == 0, row_ref[...], 0.0), axis=1, keepdims=True), (8, 128))
    scale = descent_rate * lax.rsqrt(squares * (1.0 / (SPACE * LAYERS * ROWS * LANES)) + epsilon)
    for l in range(LAYERS):
        for r in range(0, ROWS, 8):
            for k in (0, 1):
                lanes = slice(128 * k, 128 * k + 128)
                out_ref[l, r : r + 8, lanes] = mean_ref[l, r : r + 8, lanes] - scale * tot_ref[l, k, r : r + 8, :]
    misfit_ref[0, 0] = jnp.sum(jnp.where(lane == 1, row_ref[...], 0.0)) * (0.5 / (MEMBERS * NOBS * SPACE))


def shards(mean_logk, perturbation, start_conc, source_mask, control_x, observed):
    slab = (LAYERS, ROWS, LANES)
    halved = (LAYERS, 2, ROWS, 128)
    tall = (LAYERS + 2, 2, ROWS + 2 * PAD, 128)
    f32 = jnp.float32
    dma = pltpu.SemaphoreType.DMA
    hbm, anywhere = pl.BlockSpec(memory_space=pltpu.HBM), pl.BlockSpec(memory_space=pl.ANY)
    vmem, smem = pl.BlockSpec(memory_space=pltpu.VMEM), pl.BlockSpec(memory_space=pltpu.SMEM)
    piece = ROWS // MEMBERS
    pinned = [
        pltpu.with_memory_space_constraint(v, pltpu.HBM) for v in (mean_logk, perturbation, start_conc, source_mask, control_x, observed)
    ]
    total, row = pl.pallas_call(
        kernel,
        out_shape=(jax.ShapeDtypeStruct(halved, f32), jax.ShapeDtypeStruct((1, 128), f32)),
        in_specs=[hbm] * 6,
        out_specs=(anywhere, vmem),
        scratch_shapes=[
            pltpu.VMEM(slab, f32), pltpu.VMEM(slab, f32), pltpu.VMEM(slab, jnp.int32), pltpu.VMEM((ROWS, LANES), jnp.int32),
            pltpu.SMEM((1, NOBS), f32),
        ]
        + [pltpu.VMEM(tall, f32)] * 5
        + [
            pltpu.VMEM((2, 2, ROWS, 128), f32),
            pltpu.VMEM(halved, f32),
            pltpu.VMEM((2, ROWS, 128), f32),
            pltpu.VMEM((LAYERS, 4, 2, NOBS, 128), f32),
            pltpu.VMEM((LAYERS, 2, ROWS // 2, 128), f32),
            pltpu.VMEM((LAYERS, 2, ROWS // 2, 128), f32),
            pltpu.VMEM((NHI - 1, LAYERS, 2, piece, 128), f32),
            pltpu.VMEM(halved, f32),
            pltpu.VMEM((SPACE, 1, 128), f32),
            pltpu.VMEM((NHI * NLO, 1, 128), f32),
            pltpu.VMEM((2 * NX * NZ, 1, 128), f32),
        ]
        + [dma((n,)) for n in (15, 10, 10, 2, 2, 2, 4, 4, 3, 3, 3, 3, 4, 4)]
        + [dma, pltpu.SemaphoreType.REGULAR((2,))],
        compiler_params=pltpu.CompilerParams(collective_id=0, has_side_effects=True, vmem_limit_bytes=24 << 20),
        name="step",
    )(*pinned)
    updated, misfit = pl.pallas_call(
        update_kernel,
        out_shape=(jax.ShapeDtypeStruct(slab, f32), jax.ShapeDtypeStruct((1, 1), f32)),
        in_specs=[vmem, vmem, vmem],
        out_specs=(vmem, smem),
        compiler_params=pltpu.CompilerParams(vmem_limit_bytes=8 << 20),
        name="update",
    )(row, mean_logk, total)
    return updated, misfit[0, 0]


def solution(mesh):
    in_specs = (
        P("space", None, None),
        P("member", "space", None, None),
        P("member", "space", None, None),
        P("member", "space", None, None),
        P(),
        P("member", None),
    )
    out_specs = (P("space", None, None), P())
    return jax.shard_map(shards, mesh=mesh, in_specs=in_specs, out_specs=out_specs, check_vma=False)
```

```python
import jax
import jax.numpy as jnp
from jax import lax
from jax.experimental import pallas as pl
from jax.experimental.pallas import tpu as pltpu
from jax.sharding import PartitionSpec as P

MESH = pl.DeviceIdType.MESH

NOBS = 8
time_step = 0.015
dissolve_rate = 15.0
descent_rate = 0.5
epsilon = 1e-06

HALF = 0.5 * time_step
RATE = time_step * dissolve_rate
NX, NLO, NZ, NHI = 4, 2, 8, 4
SPACE, MEMBERS = NX * NLO * NZ, 2 * NHI
LAYERS, ROWS, LANES = 4, 128, 256
PAD = 8
SEG = ROWS // NOBS
BLOCK = 32
NB = ROWS // BLOCK


def kernel(
    mean_hbm, pert_hbm, conc_hbm, mask_hbm, ctrl_hbm, obs_hbm,
    tot_ref, row_ref,
    mean, pert, mask, ctrl, obs_ref, K, C, U, D, Pf, Dp, G, acc, bnd,
    sib, hsum, rs, tot, space_buf, y_buf, plane_buf,
    load_sem, halo_s, halo_r, space_sem, y_sem, plane_sem, sib_s, sib_r, rs_s, rs_r, ag_s, ag_r, sg_s, sg_r, out_sem, relay,
):
    m, s = lax.axis_index("member"), lax.axis_index("space")
    core, h = lax.rem(m, 2), m // 2
    z, yl, x = lax.rem(s, NZ), lax.rem(s // NZ, NLO), s // (NZ * NLO)

    def dev(member, space):
        return {"member": member, "space": space}

    right, left = lax.rem(s + 1, SPACE), lax.rem(s + SPACE - 1, SPACE)
    sibling = dev(m + 1 - 2 * core, s)

    def place(dx, dl, dz):
        return (lax.rem(x + dx, NX) * NLO + lax.rem(yl + dl, NLO)) * NZ + lax.rem(z + dz, NZ)

    far_x, far_z, far_h = (2, 1, 3, 0), (4, 3, 5, 2, 6, 1, 7, 0), (2, 1, 3, 0)
    plane = [(dx, dz) for dx in far_x for dz in far_z]
    space_peers = [dev(m, place(dx, dl, dz)) for dx, dz in plane for dl in (1, 0) if dx or dl or dz]
    plane_peers = [dev(m + 1 - 2 * core, place(dx, 0, dz)) for dx, dz in plane]
    plane_peers += [dev(m, place(dx, 0, dz)) for dx, dz in plane if dx or dz]
    y_peers = [dev(lax.rem(h + dh, NHI) * 2 + core, place(0, dl, 0)) for dh in far_h for dl in (1, 0) if dh or dl]

    def greet(semaphore, peers):
        for peer in peers:
            pl.semaphore_signal(semaphore, inc=1, device_id=peer, device_id_type=MESH)

    z_ring = [dev(m, place(0, 0, dz)) for dz in far_z if dz]
    x_ring = [dev(m, place(dx, 0, 0)) for dx in far_x if dx]
    h_near = [dev(lax.rem(h + dh, NHI) * 2 + core, s) for dh in (1, NHI - 1)]
    beside = [dev(m, place(0, 1, 0)), sibling]
    near = [dev(m, right), dev(m, left)] + z_ring + x_ring + h_near + beside
    inside = pl.ds(PAD, ROWS)
    edges = (0, LAYERS - 1)
    loads = {}

    def load(name, index, src, dst):
        loads[name] = pltpu.make_async_copy(src, dst, load_sem.at[index])
        loads[name].start()

    barrier = pltpu.get_barrier_semaphore()
    greet(barrier, near)
    for i, l in enumerate(edges):
        load(("m", l), i, mean_hbm.at[l], mean.at[l])
        load(("p", l), 2 + i, pert_hbm.at[0, l], pert.at[l])
    halves = (pl.ds(0, 128), pl.ds(128, 128))
    pl.semaphore_wait(barrier, len(near))

    def halo(pairs, first):
        copies = []
        for i, (low, high, at_left, at_right) in enumerate(pairs):
            for j, (src, dst, to) in enumerate(((high, at_right, right), (low, at_left, left))):
                n = first + 2 * i + j
                copies.append(
                    pltpu.make_async_remote_copy(
                        src_ref=src, dst_ref=dst, send_sem=halo_s.at[n], recv_sem=halo_r.at[n],
                        device_id=dev(m, to), device_id_type=MESH,
                    )
                )
                copies[-1].start()
        return copies

    def layers_of(ref):
        return tuple(ref.at[e, :, inside] for e in (1, LAYERS, LAYERS + 1, 0))

    halo_1 = halo(
        [
            (*(conc_hbm.at[0, l, :, lanes] for l in edges), C.at[LAYERS + 1, k, inside], C.at[0, k, inside])
            for k, lanes in enumerate(halves)
        ],
        0,
    )
    greet(relay.at[0], x_ring + h_near)

    mid = pl.ds(1, LAYERS - 2)
    load("ctrl", 8, ctrl_hbm, ctrl)
    load("m", 9, mean_hbm.at[mid], mean.at[mid])
    load("p", 10, pert_hbm.at[0, mid], pert.at[mid])
    for i, l in enumerate(edges):
        for k, lanes in enumerate(halves):
            load(("c", l, k), 4 + 2 * i + k, conc_hbm.at[0, l, :, lanes], C.at[l + 1, k, inside])
    for k, lanes in enumerate(halves):
        load(("c", k), 11 + k, conc_hbm.at[0, mid, :, lanes], C.at[pl.ds(2, LAYERS - 2), k, inside])
    load("mask", 13, mask_hbm.at[0], mask)
    load("obs", 14, obs_hbm, obs_ref)

    def own_rows(b):
        return pl.ds(pl.multiple_of(b * BLOCK, BLOCK), BLOCK)

    def at(ref, e, b, shift=0):
        start = pl.multiple_of(b * BLOCK, BLOCK) + (PAD + shift)
        return ref[e, :, pl.ds(start, BLOCK), :]

    def put(ref, e, b, value):
        ref[e, :, pl.ds(pl.multiple_of(b * BLOCK + PAD, PAD), BLOCK), :] = value

    def split(v):
        return jnp.stack([v[:, :128], v[:, 128:]])

    def shifts_z(v):
        lane = lax.broadcasted_iota(jnp.int32, v.shape, 2)
        before, after = pltpu.roll(v, 1, 2), pltpu.roll(v, 127, 2)
        zero = jnp.zeros_like(v[0])
        down = jnp.where(lane == 0, jnp.stack([zero, before[0]]), before)
        up = jnp.where(lane == 127, jnp.stack([after[1], zero]), after)
        return down, up

    def neighbours(ref, e, b, beside):
        v = at(ref, e, b)
        return v, [at(ref, n, b) for n in beside] + [at(ref, e, b, -1), at(ref, e, b, 1), *shifts_z(v)]

    def each(layers, body):
        first, step, count = layers

        def run(i, carry):
            body(first + step * (i // NB), lax.rem(i, NB))
            return carry

        lax.fori_loop(0, count * NB, run, 0)

    OUTER, INNER, OWN = (1, LAYERS - 1, 2), (2, 1, LAYERS - 2), (1, 1, LAYERS)

    def conductivity(e, b):
        put(K, e, b, split(jnp.exp(mean[e - 1, own_rows(b), :] + pert[e - 1, own_rows(b), :])))

    def selected(e, b):
        where_x = s * LAYERS + (e - 1)
        put(U, e, b, jnp.where(split(ctrl[own_rows(b), :]) == where_x, at(K, e, b), 0.0))

    def edge_of(e):
        return (e - 1) // (LAYERS - 1)

    def inner_of(e):
        return 2 + edge_of(e) * (LAYERS - 3), edge_of(e) * (LAYERS + 1)

    def rate_of(e, b):
        return RATE * split(mask[e - 1, own_rows(b), :]).astype(jnp.float32)

    def gather_discharge(e, b, first, adj, u):
        acc[:, own_rows(b), :] += adj * first + u * rate_of(e, b)

    def transport_block(e, b, beside):
        k, ks = neighbours(K, e, b, beside)
        c, cs = neighbours(C, e, b, beside)
        u, us = neighbours(U, e, b, beside)
        flow_c, flow_u = jnp.zeros_like(c), jnp.zeros_like(u)
        for kn, cn, un in zip(ks, cs, us):
            face = k + kn
            flow_c, flow_u = flow_c + face * (cn - c), flow_u + face * (un - u)
        rate = rate_of(e, b)
        first = c + HALF * flow_c + rate * (1.0 - c)
        adj = u + HALF * flow_u - rate * u
        put(Pf, e, b, adj)
        return first, adj, u

    def transport_inner(e, b):
        first, adj, u = transport_block(e, b, (e - 1, e + 1))
        put(D, e, b, first)
        gather_discharge(e, b, first, adj, u)

    def transport_outer(e, b):
        Dp[edge_of(e), :, own_rows(b), :] = transport_block(e, b, (inner_of(e)[0],))[0]

    def transport_halo(e, b):
        n = inner_of(e)[1]
        face = HALF * (at(K, e, b) + at(K, n, b))
        u = at(U, e, b)
        first = Dp[edge_of(e), :, own_rows(b), :] + face * (at(C, n, b) - at(C, e, b))
        adj = at(Pf, e, b) + face * (at(U, n, b) - u)
        put(D, e, b, first)
        put(Pf, e, b, adj)
        gather_discharge(e, b, first, adj, u)

    def gradient_block(e, b, beside):
        fields = [neighbours(ref, e, b, beside) for ref in (K, C, U, D, Pf)]
        k, c, u, d, p = (centre for centre, _ in fields)
        flow_d, bracket = jnp.zeros_like(d), jnp.zeros_like(d)
        for kn, cn, un, dn, pn in zip(*(around for _, around in fields)):
            slope = dn - d
            flow_d = flow_d + (k + kn) * slope
            bracket = bracket + ((un - u) * slope + (pn - p) * (cn - c))
        second = d + HALF * flow_d + rate_of(e, b) * (1.0 - d)
        G[e - 1, :, own_rows(b), :] = u * second - HALF * k * bracket

    def gradient_inner(e, b):
        gradient_block(e, b, (e - 1, e + 1))

    def gradient_outer(e, b):
        gradient_block(e, b, (inner_of(e)[0],))

    def gradient_halo(e, b):
        n, own = inner_of(e)[1], own_rows(b)
        k, kn, u, un = at(K, e, b), at(K, n, b), at(U, e, b), at(U, n, b)
        slope = at(C, n, b) - at(C, e, b)
        inside_grid = jnp.where(s == edge_of(e) * (SPACE - 1), 0.0, 1.0)
        dn = (at(D, n, b) - HALF * (k + kn) * slope) * inside_grid
        by_d = (dn - at(D, e, b)) * (u * (k + kn) - k * (un - u))
        by_c = k * (at(Pf, n, b) * inside_grid - at(Pf, e, b)) * slope
        G[e - 1, :, own, :] += HALF * (by_d - by_c)

    SIDES = ((0, -1, 1), (SEG - 1, SEG, SEG - 2))

    def strided(ref, e, row):
        return ref[e, :, pl.ds(PAD + row, NOBS, stride=SEG), :]

    def crossing(e, side):
        own_row, over, _ = side
        return HALF * (strided(K, e, own_row) + strided(K, e, over)) * strided(U, e, over)

    def crossing_terms(e):
        return [crossing(e, side) * strided(D, e, side[0]) for side in SIDES]

    def boundary_gradient(e):
        for i, side in enumerate(SIDES):
            row, over, further = side
            q, k, c = crossing(e, side), strided(K, e, row), strided(C, e, row)
            u_over, c_over, c_further = strided(U, e, over), strided(C, e, over), strided(C, e, further)
            p_over = strided(Pf, e, over) - HALF * (k + strided(K, e, over)) * strided(U, e, row)
            bracket = u_over * (strided(D, e, over) - strided(D, e, row))
            bracket += (p_over - q) * (c_over - c) - q * (c_further - c)
            for n in (e - 1, e + 1):
                bracket += (crossing(n, side) - q) * (strided(C, n, row) - c)
            for qn, cn in zip(shifts_z(q), shifts_z(c)):
                bracket += (qn - q) * (cn - c)
            bnd[e - 1, 2 * i] = -HALF * k * bracket
            bnd[e - 1, 2 * i + 1] = -HALF * strided(K, e, further) * (q * (c - c_further))

    for l in edges:
        loads[("m", l)].wait()
        loads[("p", l)].wait()
    each(OUTER, conductivity)
    halo_1 += halo((layers_of(K),), 4)

    zero_rows = jnp.zeros((2, PAD, 128), jnp.float32)
    for ref in (K, C, U, D, Pf):
        for e in range(LAYERS + 2):
            ref[e, :, 0:PAD, :] = zero_rows
            ref[e, :, PAD + ROWS : 2 * PAD + ROWS, :] = zero_rows
    acc[...] = jnp.zeros_like(acc)
    loads["m"].wait()
    loads["p"].wait()
    each(INNER, conductivity)
    pl.semaphore_wait(relay.at[0], len(x_ring + h_near))
    greet(relay.at[1], beside)
    loads["ctrl"].wait()
    each(OWN, selected)
    for l in edges:
        for k in (0, 1):
            loads[("c", l, k)].wait()
    for k in (0, 1):
        loads[("c", k)].wait()
    loads["mask"].wait()
    loads["obs"].wait()
    each(OUTER, transport_outer)
    each(INNER, transport_inner)
    for copy in halo_1:
        copy.wait_send()
    halo_2 = halo(((Dp.at[0], Dp.at[1], *layers_of(D)[2:]),), 6)
    cross_in = [crossing_terms(e) for e in range(2, LAYERS)]

    def clear(refs):
        blank = jnp.zeros((2, ROWS, 128), jnp.float32)

        @pl.when(s == 0)
        def _():
            for ref in refs:
                ref[0, :, PAD : PAD + ROWS, :] = blank

        @pl.when(s == SPACE - 1)
        def _():
            for ref in refs:
                ref[LAYERS + 1, :, PAD : PAD + ROWS, :] = blank

    for copy in halo_1:
        copy.wait_recv()
    clear((K, C))
    each((0, LAYERS + 1, 2), selected)
    each(OUTER, transport_halo)

    eye = (lax.broadcasted_iota(jnp.int32, (NOBS, 128), 0) == lax.broadcasted_iota(jnp.int32, (NOBS, 128), 1)).astype(jnp.float32)
    sub = lax.broadcasted_iota(jnp.int32, (NOBS, 128), 0)
    parts = acc[:, pl.ds(0, NOBS, stride=SEG), :]
    for i in range(1, SEG):
        parts = parts + acc[:, pl.ds(i, NOBS, stride=SEG), :]
    cross_all = cross_in + [crossing_terms(1), crossing_terms(LAYERS)]
    lower, upper = (sum(terms[i] for terms in cross_all) for i in (0, 1))
    parts = parts - lower - upper + pltpu.roll(lower, NOBS - 1, 1) + pltpu.roll(upper, 1, 1)
    column = jnp.sum(parts[0] + parts[1], axis=1, keepdims=True)

    def to_row(column):
        return jnp.sum(eye * column, axis=0, keepdims=True)

    def exchange(buf, slot, row, peers, sems):
        buf[slot] = row
        for peer in peers:
            pltpu.make_async_remote_copy(
                src_ref=buf.at[slot], dst_ref=buf.at[slot],
                send_sem=sems.at[0], recv_sem=sems.at[1],
                device_id=peer, device_id_type=MESH,
            ).start()

    def finish(buf, count, sems):
        span = buf.at[pl.ds(0, count)]
        pltpu.make_async_copy(span, span, sems.at[1]).wait()
        pltpu.make_async_copy(span, span, sems.at[0]).wait()
        return jnp.sum(buf[...], axis=0)

    pl.semaphore_wait(relay.at[1], len(beside))
    exchange(space_buf, s, to_row(column), space_peers, space_sem)
    halo_2 += halo((layers_of(Pf),), 8)

    each(INNER, gradient_inner)
    each(OUTER, gradient_outer)
    for e in range(2, LAYERS):
        boundary_gradient(e)
    for copy in halo_2:
        copy.wait_recv()
    each(OUTER, gradient_halo)
    boundary_gradient(1)
    boundary_gradient(LAYERS)
    row = finish(space_buf, SPACE - 1, space_sem)

    observed = jnp.zeros((NOBS, 128), jnp.float32)
    for j in range(NOBS):
        observed = jnp.where(sub == j, obs_ref[0, j], observed)
    total_column = jnp.sum(eye * row, axis=1, keepdims=True)
    resid = total_column * (1.0 / (ROWS * LANES // NOBS)) - observed
    misfit = jnp.sum(resid * resid, axis=0, keepdims=True)
    below = jnp.where(sub == 0, 0.0, pltpu.roll(resid, 1, 0) - resid)
    above = jnp.where(sub == NOBS - 1, 0.0, pltpu.roll(resid, NOBS - 1, 0) - resid)
    deltas = (below, above)

    def weigh(l, carry):
        for half in (0, 1):
            for j in range(NOBS):
                rows = pl.ds(j * SEG, SEG)
                G[l, half, rows, :] = G[l, half, rows, :] * jnp.broadcast_to(resid[j : j + 1], (SEG, 128))
            for i, (row, _, further) in enumerate(SIDES):
                for k, r in enumerate((row, further)):
                    where = pl.ds(r, NOBS, stride=SEG)
                    G[l, half, where, :] = G[l, half, where, :] + deltas[i] * bnd[l, 2 * i + k, half]
        return carry

    lax.fori_loop(0, LAYERS, weigh, 0)

    half_rows = ROWS // 2
    piece = half_rows // NHI

    def piece_of(chip):
        return pl.ds(pl.multiple_of(chip * piece, piece), piece)

    def rows_of(of_core, chip):
        return pl.ds(pl.multiple_of(of_core * half_rows + chip * piece, piece), piece)

    order = (2, 1, 3, 0)
    cores = []
    for i, k in enumerate(order):
        chip = lax.rem(h + k, NHI)
        cores.append(
            pltpu.make_async_remote_copy(
                src_ref=G.at[:, :, rows_of(1 - core, chip), :], dst_ref=sib.at[:, :, piece_of(chip), :],
                send_sem=sib_s.at[i], recv_sem=sib_r.at[i], device_id=sibling, device_id_type=MESH,
            )
        )
        cores[-1].start()
    parts_of = (pl.ds(0, LAYERS // 2), pl.ds(LAYERS // 2, LAYERS // 2))
    scatter = ([], [])

    def send_part(q, i, chip):
        copy = pltpu.make_async_remote_copy(
            src_ref=hsum.at[parts_of[q], :, piece_of(chip), :], dst_ref=rs.at[i, parts_of[q]],
            send_sem=rs_s.at[3 * q + i], recv_sem=rs_r.at[3 * q + i],
            device_id=dev(chip * 2 + core, s), device_id_type=MESH,
        )
        copy.start()
        scatter[q].append(copy)

    for i, k in enumerate(order):
        chip = lax.rem(h + k, NHI)
        cores[i].wait_recv()
        hsum[:, :, piece_of(chip), :] = G[:, :, rows_of(core, chip), :] + sib[:, :, piece_of(chip), :]
        if k:
            send_part(0, i, chip)
    for i, k in enumerate(order):
        if k:
            send_part(1, i, lax.rem(h + k, NHI))

    def hand_on(q, chip, i):
        part = tot.at[parts_of[q], :, rows_of(core, chip), :]
        copy = pltpu.make_async_remote_copy(
            src_ref=part, dst_ref=part, send_sem=sg_s.at[4 * q + i], recv_sem=sg_r.at[4 * q + i],
            device_id=sibling, device_id_type=MESH,
        )
        copy.start()
        return copy

    gather, handed = ([], []), []
    squares = jnp.zeros((piece, 128), jnp.float32)
    for q in (0, 1):
        for copy in scatter[q]:
            copy.wait_recv()
        total = hsum[parts_of[q], :, piece_of(h), :] + rs[0, parts_of[q]] + rs[1, parts_of[q]] + rs[2, parts_of[q]]
        tot[parts_of[q], :, rows_of(core, h), :] = total
        mine = tot.at[parts_of[q], :, rows_of(core, h), :]
        for i, k in enumerate((2, 1, 3)):
            copy = pltpu.make_async_remote_copy(
                src_ref=mine, dst_ref=mine, send_sem=ag_s.at[3 * q + i], recv_sem=ag_r.at[3 * q + i],
                device_id=dev(lax.rem(h + k, NHI) * 2 + core, s), device_id_type=MESH,
            )
            copy.start()
            gather[q].append(copy)
        handed.append(hand_on(q, h, 0))
        squares = squares + jnp.sum(total * total, axis=(0, 1))

    squares = jnp.sum(squares, axis=0, keepdims=True)
    squares = jnp.sum(squares, axis=1, keepdims=True)
    lane_row = lax.broadcasted_iota(jnp.int32, (1, 128), 1)
    row = jnp.where(lane_row == 0, squares, jnp.where(lane_row == 1, misfit, 0.0))
    exchange(plane_buf, (x * NZ + z) * 2 + core, row, plane_peers, plane_sem)
    row = finish(plane_buf, 2 * NX * NZ - 1, plane_sem)
    exchange(y_buf, h * NLO + yl, row, y_peers, y_sem)

    for q in (0, 1):
        for i, k in ((1, 1), (2, 3), (0, 2)):
            gather[q][i].wait_recv()
            handed.append(hand_on(q, lax.rem(h + NHI - k, NHI), i + 1))
    for copy in handed:
        copy.wait_recv()
    out = pltpu.make_async_copy(tot, tot_ref, out_sem)
    out.start()
    for copy in halo_2 + cores + scatter[0] + scatter[1] + gather[0] + gather[1] + handed:
        copy.wait_send()
    row = finish(y_buf, NHI * NLO - 1, y_sem)
    row_ref[...] = row
    out.wait()


def update_kernel(row_ref, mean_ref, tot_ref, out_ref, misfit_ref):
    lane = lax.broadcasted_iota(jnp.int32, (1, 128), 1)
    squares = jnp.broadcast_to(jnp.sum(jnp.where(lane == 0, row_ref[...], 0.0), axis=1, keepdims=True), (8, 128))
    scale = descent_rate * lax.rsqrt(squares * (1.0 / (SPACE * LAYERS * ROWS * LANES)) + epsilon)
    for l in range(LAYERS):
        for r in range(0, ROWS, 8):
            for k in (0, 1):
                lanes = slice(128 * k, 128 * k + 128)
                out_ref[l, r : r + 8, lanes] = mean_ref[l, r : r + 8, lanes] - scale * tot_ref[l, k, r : r + 8, :]
    misfit_ref[0, 0] = jnp.sum(jnp.where(lane == 1, row_ref[...], 0.0)) * (0.5 / (MEMBERS * NOBS * SPACE))


def shards(mean_logk, perturbation, start_conc, source_mask, control_x, observed):
    slab = (LAYERS, ROWS, LANES)
    halved = (LAYERS, 2, ROWS, 128)
    tall = (LAYERS + 2, 2, ROWS + 2 * PAD, 128)
    f32 = jnp.float32
    dma = pltpu.SemaphoreType.DMA
    hbm, anywhere = pl.BlockSpec(memory_space=pltpu.HBM), pl.BlockSpec(memory_space=pl.ANY)
    vmem, smem = pl.BlockSpec(memory_space=pltpu.VMEM), pl.BlockSpec(memory_space=pltpu.SMEM)
    piece = ROWS // MEMBERS
    pinned = [
        pltpu.with_memory_space_constraint(v, pltpu.HBM) for v in (mean_logk, perturbation, start_conc, source_mask, control_x, observed)
    ]
    total, row = pl.pallas_call(
        kernel,
        out_shape=(jax.ShapeDtypeStruct(halved, f32), jax.ShapeDtypeStruct((1, 128), f32)),
        in_specs=[hbm] * 6,
        out_specs=(anywhere, vmem),
        scratch_shapes=[
            pltpu.VMEM(slab, f32), pltpu.VMEM(slab, f32), pltpu.VMEM(slab, jnp.int32), pltpu.VMEM((ROWS, LANES), jnp.int32),
            pltpu.SMEM((1, NOBS), f32),
        ]
        + [pltpu.VMEM(tall, f32)] * 5
        + [
            pltpu.VMEM((2, 2, ROWS, 128), f32),
            pltpu.VMEM(halved, f32),
            pltpu.VMEM((2, ROWS, 128), f32),
            pltpu.VMEM((LAYERS, 4, 2, NOBS, 128), f32),
            pltpu.VMEM((LAYERS, 2, ROWS // 2, 128), f32),
            pltpu.VMEM((LAYERS, 2, ROWS // 2, 128), f32),
            pltpu.VMEM((NHI - 1, LAYERS, 2, piece, 128), f32),
            pltpu.VMEM(halved, f32),
            pltpu.VMEM((SPACE, 1, 128), f32),
            pltpu.VMEM((NHI * NLO, 1, 128), f32),
            pltpu.VMEM((2 * NX * NZ, 1, 128), f32),
        ]
        + [dma((n,)) for n in (15, 10, 10, 2, 2, 2, 4, 4, 6, 6, 6, 6, 8, 8)]
        + [dma, pltpu.SemaphoreType.REGULAR((2,))],
        compiler_params=pltpu.CompilerParams(collective_id=0, has_side_effects=True, vmem_limit_bytes=24 << 20),
        name="step",
    )(*pinned)
    updated, misfit = pl.pallas_call(
        update_kernel,
        out_shape=(jax.ShapeDtypeStruct(slab, f32), jax.ShapeDtypeStruct((1, 1), f32)),
        in_specs=[vmem, vmem, vmem],
        out_specs=(vmem, smem),
        compiler_params=pltpu.CompilerParams(vmem_limit_bytes=8 << 20),
        name="update",
    )(row, mean_logk, total)
    return updated, misfit[0, 0]


def solution(mesh):
    in_specs = (
        P("space", None, None),
        P("member", "space", None, None),
        P("member", "space", None, None),
        P("member", "space", None, None),
        P(),
        P("member", None),
    )
    out_specs = (P("space", None, None), P())
    return jax.shard_map(shards, mesh=mesh, in_specs=in_specs, out_specs=out_specs, check_vma=False)
```

```python
import jax
import jax.numpy as jnp
from jax import lax
from jax.experimental import pallas as pl
from jax.experimental.pallas import tpu as pltpu
from jax.sharding import PartitionSpec as P

MESH = pl.DeviceIdType.MESH

NOBS = 8
time_step = 0.015
dissolve_rate = 15.0
descent_rate = 0.5
epsilon = 1e-06

HALF = 0.5 * time_step
RATE = time_step * dissolve_rate
NX, NLO, NZ, NHI = 4, 2, 8, 4
SPACE, MEMBERS = NX * NLO * NZ, 2 * NHI
LAYERS, ROWS, LANES = 4, 128, 256
PAD = 8
SEG = ROWS // NOBS
BLOCK = 32
NB = ROWS // BLOCK


def kernel(
    mean_hbm, pert_hbm, conc_hbm, mask_hbm, ctrl_hbm, obs_hbm,
    tot_ref, row_ref,
    mean, pert, mask, ctrl, obs_ref, K, C, U, D, Pf, Dp, G, acc, bnd,
    sib, hsum, rs, tot, space_buf, y_buf, plane_buf,
    load_sem, halo_s, halo_r, space_sem, y_sem, plane_sem, sib_s, sib_r, rs_s, rs_r, ag_s, ag_r, sg_s, sg_r, out_sem, relay,
):
    m, s = lax.axis_index("member"), lax.axis_index("space")
    core, h = lax.rem(m, 2), m // 2
    z, yl, x = lax.rem(s, NZ), lax.rem(s // NZ, NLO), s // (NZ * NLO)

    def dev(member, space):
        return {"member": member, "space": space}

    right, left = lax.rem(s + 1, SPACE), lax.rem(s + SPACE - 1, SPACE)
    sibling = dev(m + 1 - 2 * core, s)

    def place(dx, dl, dz):
        return (lax.rem(x + dx, NX) * NLO + lax.rem(yl + dl, NLO)) * NZ + lax.rem(z + dz, NZ)

    far_x, far_z, far_h = (2, 1, 3, 0), (4, 3, 5, 2, 6, 1, 7, 0), (2, 1, 3, 0)
    plane = [(dx, dz) for dx in far_x for dz in far_z]
    space_peers = [dev(m, place(dx, dl, dz)) for dx, dz in plane for dl in (1, 0) if dx or dl or dz]
    plane_peers = [dev(m + 1 - 2 * core, place(dx, 0, dz)) for dx, dz in plane]
    plane_peers += [dev(m, place(dx, 0, dz)) for dx, dz in plane if dx or dz]
    y_peers = [dev(lax.rem(h + dh, NHI) * 2 + core, place(0, dl, 0)) for dh in far_h for dl in (1, 0) if dh or dl]

    def greet(semaphore, peers):
        for peer in peers:
            pl.semaphore_signal(semaphore, inc=1, device_id=peer, device_id_type=MESH)

    z_ring = [dev(m, place(0, 0, dz)) for dz in far_z if dz]
    x_ring = [dev(m, place(dx, 0, 0)) for dx in far_x if dx]
    h_near = [dev(lax.rem(h + dh, NHI) * 2 + core, s) for dh in (1, NHI - 1)]
    beside = [dev(m, place(0, 1, 0)), sibling]
    near = [dev(m, right), dev(m, left)] + z_ring + x_ring + h_near + beside
    inside = pl.ds(PAD, ROWS)
    edges = (0, LAYERS - 1)
    loads = {}

    def load(name, index, src, dst):
        loads[name] = pltpu.make_async_copy(src, dst, load_sem.at[index])
        loads[name].start()

    barrier = pltpu.get_barrier_semaphore()
    greet(barrier, near)
    for i, l in enumerate(edges):
        load(("m", l), i, mean_hbm.at[l], mean.at[l])
        load(("p", l), 2 + i, pert_hbm.at[0, l], pert.at[l])
    halves = (pl.ds(0, 128), pl.ds(128, 128))
    pl.semaphore_wait(barrier, len(near))

    def halo(pairs, first):
        copies = []
        for i, (low, high, at_left, at_right) in enumerate(pairs):
            for j, (src, dst, to) in enumerate(((high, at_right, right), (low, at_left, left))):
                n = first + 2 * i + j
                copies.append(
                    pltpu.make_async_remote_copy(
                        src_ref=src, dst_ref=dst, send_sem=halo_s.at[n], recv_sem=halo_r.at[n],
                        device_id=dev(m, to), device_id_type=MESH,
                    )
                )
                copies[-1].start()
        return copies

    def layers_of(ref):
        return tuple(ref.at[e, :, inside] for e in (1, LAYERS, LAYERS + 1, 0))

    halo_1 = halo(
        [
            (*(conc_hbm.at[0, l, :, lanes] for l in edges), C.at[LAYERS + 1, k, inside], C.at[0, k, inside])
            for k, lanes in enumerate(halves)
        ],
        0,
    )
    greet(relay.at[0], x_ring + h_near)

    mid = pl.ds(1, LAYERS - 2)
    load("ctrl", 8, ctrl_hbm, ctrl)
    load("m", 9, mean_hbm.at[mid], mean.at[mid])
    load("p", 10, pert_hbm.at[0, mid], pert.at[mid])
    for i, l in enumerate(edges):
        for k, lanes in enumerate(halves):
            load(("c", l, k), 4 + 2 * i + k, conc_hbm.at[0, l, :, lanes], C.at[l + 1, k, inside])
    for k, lanes in enumerate(halves):
        load(("c", k), 11 + k, conc_hbm.at[0, mid, :, lanes], C.at[pl.ds(2, LAYERS - 2), k, inside])
    load("mask", 13, mask_hbm.at[0], mask)
    load("obs", 14, obs_hbm, obs_ref)

    def own_rows(b):
        return pl.ds(pl.multiple_of(b * BLOCK, BLOCK), BLOCK)

    def at(ref, e, b, shift=0):
        start = pl.multiple_of(b * BLOCK, BLOCK) + (PAD + shift)
        return ref[e, :, pl.ds(start, BLOCK), :]

    def put(ref, e, b, value):
        ref[e, :, pl.ds(pl.multiple_of(b * BLOCK + PAD, PAD), BLOCK), :] = value

    def split(v):
        return jnp.stack([v[:, :128], v[:, 128:]])

    def shifts_z(v):
        lane = lax.broadcasted_iota(jnp.int32, v.shape, 2)
        before, after = pltpu.roll(v, 1, 2), pltpu.roll(v, 127, 2)
        zero = jnp.zeros_like(v[0])
        down = jnp.where(lane == 0, jnp.stack([zero, before[0]]), before)
        up = jnp.where(lane == 127, jnp.stack([after[1], zero]), after)
        return down, up

    def neighbours(ref, e, b, beside):
        v = at(ref, e, b)
        return v, [at(ref, n, b) for n in beside] + [at(ref, e, b, -1), at(ref, e, b, 1), *shifts_z(v)]

    def each(layers, body):
        first, step, count = layers

        def run(i, carry):
            body(first + step * (i // NB), lax.rem(i, NB))
            return carry

        lax.fori_loop(0, count * NB, run, 0)

    OUTER, INNER, OWN = (1, LAYERS - 1, 2), (2, 1, LAYERS - 2), (1, 1, LAYERS)

    def conductivity(e, b):
        put(K, e, b, split(jnp.exp(mean[e - 1, own_rows(b), :] + pert[e - 1, own_rows(b), :])))

    def selected(e, b):
        where_x = s * LAYERS + (e - 1)
        put(U, e, b, jnp.where(split(ctrl[own_rows(b), :]) == where_x, at(K, e, b), 0.0))

    def edge_of(e):
        return (e - 1) // (LAYERS - 1)

    def inner_of(e):
        return 2 + edge_of(e) * (LAYERS - 3), edge_of(e) * (LAYERS + 1)

    def rate_of(e, b):
        return RATE * split(mask[e - 1, own_rows(b), :]).astype(jnp.float32)

    def gather_discharge(e, b, first, adj, u):
        acc[:, own_rows(b), :] += adj * first + u * rate_of(e, b)

    def transport_block(e, b, beside):
        k, ks = neighbours(K, e, b, beside)
        c, cs = neighbours(C, e, b, beside)
        u, us = neighbours(U, e, b, beside)
        flow_c, flow_u = jnp.zeros_like(c), jnp.zeros_like(u)
        for kn, cn, un in zip(ks, cs, us):
            face = k + kn
            flow_c, flow_u = flow_c + face * (cn - c), flow_u + face * (un - u)
        rate = rate_of(e, b)
        first = c + HALF * flow_c + rate * (1.0 - c)
        adj = u + HALF * flow_u - rate * u
        put(Pf, e, b, adj)
        return first, adj, u

    def transport_inner(e, b):
        first, adj, u = transport_block(e, b, (e - 1, e + 1))
        put(D, e, b, first)
        gather_discharge(e, b, first, adj, u)

    def transport_outer(e, b):
        Dp[edge_of(e), :, own_rows(b), :] = transport_block(e, b, (inner_of(e)[0],))[0]

    def transport_halo(e, b):
        n = inner_of(e)[1]
        face = HALF * (at(K, e, b) + at(K, n, b))
        u = at(U, e, b)
        first = Dp[edge_of(e), :, own_rows(b), :] + face * (at(C, n, b) - at(C, e, b))
        adj = at(Pf, e, b) + face * (at(U, n, b) - u)
        put(D, e, b, first)
        put(Pf, e, b, adj)
        gather_discharge(e, b, first, adj, u)

    def gradient_block(e, b, beside):
        fields = [neighbours(ref, e, b, beside) for ref in (K, C, U, D, Pf)]
        k, c, u, d, p = (centre for centre, _ in fields)
        flow_d, bracket = jnp.zeros_like(d), jnp.zeros_like(d)
        for kn, cn, un, dn, pn in zip(*(around for _, around in fields)):
            slope = dn - d
            flow_d = flow_d + (k + kn) * slope
            bracket = bracket + ((un - u) * slope + (pn - p) * (cn - c))
        second = d + HALF * flow_d + rate_of(e, b) * (1.0 - d)
        G[e - 1, :, own_rows(b), :] = u * second - HALF * k * bracket

    def gradient_inner(e, b):
        gradient_block(e, b, (e - 1, e + 1))

    def gradient_outer(e, b):
        gradient_block(e, b, (inner_of(e)[0],))

    def gradient_halo(e, b):
        n, own = inner_of(e)[1], own_rows(b)
        k, kn, u, un = at(K, e, b), at(K, n, b), at(U, e, b), at(U, n, b)
        slope = at(C, n, b) - at(C, e, b)
        inside_grid = jnp.where(s == edge_of(e) * (SPACE - 1), 0.0, 1.0)
        dn = (at(D, n, b) - HALF * (k + kn) * slope) * inside_grid
        by_d = (dn - at(D, e, b)) * (u * (k + kn) - k * (un - u))
        by_c = k * (at(Pf, n, b) * inside_grid - at(Pf, e, b)) * slope
        G[e - 1, :, own, :] += HALF * (by_d - by_c)

    SIDES = ((0, -1, 1), (SEG - 1, SEG, SEG - 2))

    def strided(ref, e, row):
        return ref[e, :, pl.ds(PAD + row, NOBS, stride=SEG), :]

    def crossing(e, side):
        own_row, over, _ = side
        return HALF * (strided(K, e, own_row) + strided(K, e, over)) * strided(U, e, over)

    def crossing_terms(e):
        return [crossing(e, side) * strided(D, e, side[0]) for side in SIDES]

    def boundary_gradient(e):
        for i, side in enumerate(SIDES):
            row, over, further = side
            q, k, c = crossing(e, side), strided(K, e, row), strided(C, e, row)
            u_over, c_over, c_further = strided(U, e, over), strided(C, e, over), strided(C, e, further)
            p_over = strided(Pf, e, over) - HALF * (k + strided(K, e, over)) * strided(U, e, row)
            bracket = u_over * (strided(D, e, over) - strided(D, e, row))
            bracket += (p_over - q) * (c_over - c) - q * (c_further - c)
            for n in (e - 1, e + 1):
                bracket += (crossing(n, side) - q) * (strided(C, n, row) - c)
            for qn, cn in zip(shifts_z(q), shifts_z(c)):
                bracket += (qn - q) * (cn - c)
            bnd[e - 1, 2 * i] = -HALF * k * bracket
            bnd[e - 1, 2 * i + 1] = -HALF * strided(K, e, further) * (q * (c - c_further))

    low, high, at_left, at_right = layers_of(K)
    for n, e, src, dst, to in ((4, LAYERS, high, at_right, right), (5, 1, low, at_left, left)):
        loads[("m", e - 1)].wait()
        loads[("p", e - 1)].wait()
        each((e, 1, 1), conductivity)
        halo_1.append(
            pltpu.make_async_remote_copy(
                src_ref=src, dst_ref=dst, send_sem=halo_s.at[n], recv_sem=halo_r.at[n],
                device_id=dev(m, to), device_id_type=MESH,
            )
        )
        halo_1[-1].start()

    zero_rows = jnp.zeros((2, PAD, 128), jnp.float32)
    for ref in (K, C, U, D, Pf):
        for e in range(LAYERS + 2):
            ref[e, :, 0:PAD, :] = zero_rows
            ref[e, :, PAD + ROWS : 2 * PAD + ROWS, :] = zero_rows
    acc[...] = jnp.zeros_like(acc)
    loads["m"].wait()
    loads["p"].wait()
    each(INNER, conductivity)
    pl.semaphore_wait(relay.at[0], len(x_ring + h_near))
    greet(relay.at[1], beside)
    loads["ctrl"].wait()
    each(OWN, selected)
    for l in edges:
        for k in (0, 1):
            loads[("c", l, k)].wait()
    for k in (0, 1):
        loads[("c", k)].wait()
    loads["mask"].wait()
    loads["obs"].wait()
    each(OUTER, transport_outer)
    each(INNER, transport_inner)
    for copy in halo_1:
        copy.wait_send()
    halo_2 = halo(((Dp.at[0], Dp.at[1], *layers_of(D)[2:]),), 6)
    cross_in = [crossing_terms(e) for e in range(2, LAYERS)]

    def clear(refs):
        blank = jnp.zeros((2, ROWS, 128), jnp.float32)

        @pl.when(s == 0)
        def _():
            for ref in refs:
                ref[0, :, PAD : PAD + ROWS, :] = blank

        @pl.when(s == SPACE - 1)
        def _():
            for ref in refs:
                ref[LAYERS + 1, :, PAD : PAD + ROWS, :] = blank

    for copy in halo_1:
        copy.wait_recv()
    clear((K, C))
    each((0, LAYERS + 1, 2), selected)
    each(OUTER, transport_halo)

    eye = (lax.broadcasted_iota(jnp.int32, (NOBS, 128), 0) == lax.broadcasted_iota(jnp.int32, (NOBS, 128), 1)).astype(jnp.float32)
    sub = lax.broadcasted_iota(jnp.int32, (NOBS, 128), 0)
    parts = acc[:, pl.ds(0, NOBS, stride=SEG), :]
    for i in range(1, SEG):
        parts = parts + acc[:, pl.ds(i, NOBS, stride=SEG), :]
    cross_all = cross_in + [crossing_terms(1), crossing_terms(LAYERS)]
    lower, upper = (sum(terms[i] for terms in cross_all) for i in (0, 1))
    parts = parts - lower - upper + pltpu.roll(lower, NOBS - 1, 1) + pltpu.roll(upper, 1, 1)
    column = jnp.sum(parts[0] + parts[1], axis=1, keepdims=True)

    def to_row(column):
        return jnp.sum(eye * column, axis=0, keepdims=True)

    def exchange(buf, slot, row, peers, sems):
        buf[slot] = row
        for peer in peers:
            pltpu.make_async_remote_copy(
                src_ref=buf.at[slot], dst_ref=buf.at[slot],
                send_sem=sems.at[0], recv_sem=sems.at[1],
                device_id=peer, device_id_type=MESH,
            ).start()

    def finish(buf, count, sems):
        span = buf.at[pl.ds(0, count)]
        pltpu.make_async_copy(span, span, sems.at[1]).wait()
        pltpu.make_async_copy(span, span, sems.at[0]).wait()
        return jnp.sum(buf[...], axis=0)

    pl.semaphore_wait(relay.at[1], len(beside))
    exchange(space_buf, s, to_row(column), space_peers, space_sem)
    halo_2 += halo((layers_of(Pf),), 8)

    each(INNER, gradient_inner)
    each(OUTER, gradient_outer)
    for e in range(2, LAYERS):
        boundary_gradient(e)
    for copy in halo_2:
        copy.wait_recv()
    each(OUTER, gradient_halo)
    boundary_gradient(1)
    boundary_gradient(LAYERS)
    row = finish(space_buf, SPACE - 1, space_sem)

    observed = jnp.zeros((NOBS, 128), jnp.float32)
    for j in range(NOBS):
        observed = jnp.where(sub == j, obs_ref[0, j], observed)
    total_column = jnp.sum(eye * row, axis=1, keepdims=True)
    resid = total_column * (1.0 / (ROWS * LANES // NOBS)) - observed
    misfit = jnp.sum(resid * resid, axis=0, keepdims=True)
    below = jnp.where(sub == 0, 0.0, pltpu.roll(resid, 1, 0) - resid)
    above = jnp.where(sub == NOBS - 1, 0.0, pltpu.roll(resid, NOBS - 1, 0) - resid)
    deltas = (below, above)

    def weigh(l, carry):
        for half in (0, 1):
            for j in range(NOBS):
                rows = pl.ds(j * SEG, SEG)
                G[l, half, rows, :] = G[l, half, rows, :] * jnp.broadcast_to(resid[j : j + 1], (SEG, 128))
            for i, (row, _, further) in enumerate(SIDES):
                for k, r in enumerate((row, further)):
                    where = pl.ds(r, NOBS, stride=SEG)
                    G[l, half, where, :] = G[l, half, where, :] + deltas[i] * bnd[l, 2 * i + k, half]
        return carry

    lax.fori_loop(0, LAYERS, weigh, 0)

    half_rows = ROWS // 2
    piece = half_rows // NHI

    def piece_of(chip):
        return pl.ds(pl.multiple_of(chip * piece, piece), piece)

    def rows_of(of_core, chip):
        return pl.ds(pl.multiple_of(of_core * half_rows + chip * piece, piece), piece)

    order = (2, 1, 3, 0)
    cores = []
    for i, k in enumerate(order):
        chip = lax.rem(h + k, NHI)
        cores.append(
            pltpu.make_async_remote_copy(
                src_ref=G.at[:, :, rows_of(1 - core, chip), :], dst_ref=sib.at[:, :, piece_of(chip), :],
                send_sem=sib_s.at[i], recv_sem=sib_r.at[i], device_id=sibling, device_id_type=MESH,
            )
        )
        cores[-1].start()
    scatter = []
    for i, k in enumerate(order):
        chip = lax.rem(h + k, NHI)
        cores[i].wait_recv()
        hsum[:, :, piece_of(chip), :] = G[:, :, rows_of(core, chip), :] + sib[:, :, piece_of(chip), :]
        if k:
            scatter.append(
                pltpu.make_async_remote_copy(
                    src_ref=hsum.at[:, :, piece_of(chip), :], dst_ref=rs.at[i],
                    send_sem=rs_s.at[i], recv_sem=rs_r.at[i],
                    device_id=dev(chip * 2 + core, s), device_id_type=MESH,
                )
            )
            scatter[-1].start()
    for copy in scatter:
        copy.wait_recv()
    total = hsum[:, :, piece_of(h), :] + rs[0] + rs[1] + rs[2]
    tot[:, :, rows_of(core, h), :] = total

    def hand_on(chip, i):
        part = tot.at[:, :, rows_of(core, chip), :]
        copy = pltpu.make_async_remote_copy(
            src_ref=part, dst_ref=part, send_sem=sg_s.at[i], recv_sem=sg_r.at[i],
            device_id=sibling, device_id_type=MESH,
        )
        copy.start()
        return copy

    gather = []
    mine = tot.at[:, :, rows_of(core, h), :]
    for i, k in enumerate((2, 1, 3)):
        gather.append(
            pltpu.make_async_remote_copy(
                src_ref=mine, dst_ref=mine, send_sem=ag_s.at[i], recv_sem=ag_r.at[i],
                device_id=dev(lax.rem(h + k, NHI) * 2 + core, s), device_id_type=MESH,
            )
        )
        gather[-1].start()
    handed = [hand_on(h, 0)]

    squares = jnp.sum(jnp.sum(total * total, axis=(0, 1)), axis=0, keepdims=True)
    squares = jnp.sum(squares, axis=1, keepdims=True)
    lane_row = lax.broadcasted_iota(jnp.int32, (1, 128), 1)
    row = jnp.where(lane_row == 0, squares, jnp.where(lane_row == 1, misfit, 0.0))
    exchange(plane_buf, (x * NZ + z) * 2 + core, row, plane_peers, plane_sem)
    row = finish(plane_buf, 2 * NX * NZ - 1, plane_sem)
    exchange(y_buf, h * NLO + yl, row, y_peers, y_sem)

    for i, k in ((1, 1), (2, 3), (0, 2)):
        gather[i].wait_recv()
        handed.append(hand_on(lax.rem(h + NHI - k, NHI), i + 1))
    for copy in handed:
        copy.wait_recv()
    out = pltpu.make_async_copy(tot, tot_ref, out_sem)
    out.start()
    for copy in halo_2 + cores + scatter + gather + handed:
        copy.wait_send()
    row = finish(y_buf, NHI * NLO - 1, y_sem)
    row_ref[...] = row
    out.wait()


def update_kernel(row_ref, mean_ref, tot_ref, out_ref, misfit_ref):
    lane = lax.broadcasted_iota(jnp.int32, (1, 128), 1)
    squares = jnp.broadcast_to(jnp.sum(jnp.where(lane == 0, row_ref[...], 0.0), axis=1, keepdims=True), (8, 128))
    scale = descent_rate * lax.rsqrt(squares * (1.0 / (SPACE * LAYERS * ROWS * LANES)) + epsilon)
    for l in range(LAYERS):
        for r in range(0, ROWS, 8):
            for k in (0, 1):
                lanes = slice(128 * k, 128 * k + 128)
                out_ref[l, r : r + 8, lanes] = mean_ref[l, r : r + 8, lanes] - scale * tot_ref[l, k, r : r + 8, :]
    misfit_ref[0, 0] = jnp.sum(jnp.where(lane == 1, row_ref[...], 0.0)) * (0.5 / (MEMBERS * NOBS * SPACE))


def shards(mean_logk, perturbation, start_conc, source_mask, control_x, observed):
    slab = (LAYERS, ROWS, LANES)
    halved = (LAYERS, 2, ROWS, 128)
    tall = (LAYERS + 2, 2, ROWS + 2 * PAD, 128)
    f32 = jnp.float32
    dma = pltpu.SemaphoreType.DMA
    hbm, anywhere = pl.BlockSpec(memory_space=pltpu.HBM), pl.BlockSpec(memory_space=pl.ANY)
    vmem, smem = pl.BlockSpec(memory_space=pltpu.VMEM), pl.BlockSpec(memory_space=pltpu.SMEM)
    piece = ROWS // MEMBERS
    pinned = [
        pltpu.with_memory_space_constraint(v, pltpu.HBM) for v in (mean_logk, perturbation, start_conc, source_mask, control_x, observed)
    ]
    total, row = pl.pallas_call(
        kernel,
        out_shape=(jax.ShapeDtypeStruct(halved, f32), jax.ShapeDtypeStruct((1, 128), f32)),
        in_specs=[hbm] * 6,
        out_specs=(anywhere, vmem),
        scratch_shapes=[
            pltpu.VMEM(slab, f32), pltpu.VMEM(slab, f32), pltpu.VMEM(slab, jnp.int32), pltpu.VMEM((ROWS, LANES), jnp.int32),
            pltpu.SMEM((1, NOBS), f32),
        ]
        + [pltpu.VMEM(tall, f32)] * 5
        + [
            pltpu.VMEM((2, 2, ROWS, 128), f32),
            pltpu.VMEM(halved, f32),
            pltpu.VMEM((2, ROWS, 128), f32),
            pltpu.VMEM((LAYERS, 4, 2, NOBS, 128), f32),
            pltpu.VMEM((LAYERS, 2, ROWS // 2, 128), f32),
            pltpu.VMEM((LAYERS, 2, ROWS // 2, 128), f32),
            pltpu.VMEM((NHI - 1, LAYERS, 2, piece, 128), f32),
            pltpu.VMEM(halved, f32),
            pltpu.VMEM((SPACE, 1, 128), f32),
            pltpu.VMEM((NHI * NLO, 1, 128), f32),
            pltpu.VMEM((2 * NX * NZ, 1, 128), f32),
        ]
        + [dma((n,)) for n in (15, 10, 10, 2, 2, 2, 4, 4, 3, 3, 3, 3, 4, 4)]
        + [dma, pltpu.SemaphoreType.REGULAR((2,))],
        compiler_params=pltpu.CompilerParams(collective_id=0, has_side_effects=True, vmem_limit_bytes=24 << 20),
        name="step",
    )(*pinned)
    updated, misfit = pl.pallas_call(
        update_kernel,
        out_shape=(jax.ShapeDtypeStruct(slab, f32), jax.ShapeDtypeStruct((1, 1), f32)),
        in_specs=[vmem, vmem, vmem],
        out_specs=(vmem, smem),
        compiler_params=pltpu.CompilerParams(vmem_limit_bytes=8 << 20),
        name="update",
    )(row, mean_logk, total)
    return updated, misfit[0, 0]


def solution(mesh):
    in_specs = (
        P("space", None, None),
        P("member", "space", None, None),
        P("member", "space", None, None),
        P("member", "space", None, None),
        P(),
        P("member", None),
    )
    out_specs = (P("space", None, None), P())
    return jax.shard_map(shards, mesh=mesh, in_specs=in_specs, out_specs=out_specs, check_vma=False)
```
